32 devices in a mesh: station: 2 (over x), tm: 16 (over z, y, core).
Axes of the slice: x: 2, y: 2, z: 4, core: 2. Of those that a mesh axis runs over, the one named last changes fastest.
Arguments:
- features: bfloat16 [524288, 256], P(('station', 'tm')), may hold values from -8 to 8
- targets: bfloat16 [524288], P(('station', 'tm')), may hold values from -6 to 6
- station_ids: int32 [524288], P(('station', 'tm')), may hold values from 0 to 127
- lead_heads: int32 [524288], P(('station', 'tm')), may hold values from 0 to 15, as said below
- station_weight: float32 [2, 128], P('station'), may hold values from 0.2 to 5
Outputs:
- leverage: float32 [524288], P(('station', 'tm'))
- zscores: float32 [16, 256], replicated
- inverse_factor: float32 [16, 256, 256], P(None, 'tm')
The draws below stay inside these ranges and needn't reach their ends.
Inputs may be any that keep to these rules, and one draw needn't show every extreme that they name: lead_heads is constant over each aligned block of 1024 rows.
All inputs are finite; a program needn't handle non-finite values.
Results may differ from the reference program's by a relative error of at most 0.008.
Values sent between devices are 32-bit elements; how exact they have to be, the bound alone decides.
A program may use at most 128 MiB of HBM per device.

```python
import math
import jax
import jax.numpy as jnp
from jax import lax

F = 256
HEADS = 16
NSTAT = 128
BLK = 1024
ROWS = 524288
N_STATION = 2


def draw_features(key, part):
    first_key = jax.random.fold_in(key, 11)
    second_key = jax.random.fold_in(key, 12)
    base = jax.random.normal(first_key, (ROWS, F), jnp.float32)
    mixing = jnp.eye(F, dtype=jnp.float32) + 0.6 * jax.random.normal(second_key, (F, F), jnp.float32) / math.sqrt(F)
    mixed = jnp.dot(base, mixing)
    return jnp.clip(mixed, -8.0, 8.0).astype(jnp.bfloat16)


def draw_lead_heads(key, part):
    per_block = jax.random.randint(jax.random.fold_in(key, 21), (ROWS // BLK,), 0, HEADS, dtype=jnp.int32)
    return jnp.repeat(per_block, BLK)


def set_ends(array, rng, smallest, high):
    longest = array.shape.index(max(array.shape))
    spots = []
    for shift in (0, 1):
        where = [jax.random.randint(jax.random.fold_in(rng, axis), (), 0, length) for axis, length in enumerate(array.shape)]
        where[longest] = (where[longest] + shift) % array.shape[longest]
        spots.append(tuple(where))
    return array.at[spots[0]].set(smallest).at[spots[1]].set(high)


def levels(own_key, shape, pieces, least, top_value):
    loudness, own = 1.0, jax.random.fold_in(own_key, 6)
    for axis_at, parts in pieces:
        draws = jnp.exp(jax.random.uniform(jax.random.fold_in(own, axis_at), (parts,), jnp.float32, least / len(pieces), top_value / len(pieces)))
        loudness = loudness * jnp.repeat(draws, shape[axis_at] // parts).reshape([-1 if axis == axis_at else 1 for axis in range(len(shape))])
    return loudness


def normal_values(key, extent, scale, limit, pieces=(), kind=jnp.bfloat16):
    loudness = levels(key, extent, pieces, -0.22, 0.18) if pieces else 1.0
    array = jax.random.normal(key, extent, jnp.float32) * scale * loudness
    return jnp.minimum(jnp.maximum(array, -limit), limit).astype(kind)


def setup_inputs(seed: int = 0) -> dict:
    key_of = jax.random.split(jax.random.key(seed), 6)
    features = draw_features(jax.random.fold_in(key_of[5], 71), 0)
    targets = normal_values(key_of[1], (ROWS,), 1.0, 6.0, ((0, 32),))
    station_ids = set_ends(jax.random.randint(key_of[2], (ROWS,), 0, NSTAT), jax.random.fold_in(key_of[2], 1), 0, NSTAT - 1).astype(jnp.int32)
    lead_heads = draw_lead_heads(jax.random.fold_in(key_of[5], 71), 0)
    station_weight = jnp.clip(jnp.exp(math.log(5.0) - 3.218876 * jax.random.uniform(key_of[4], (N_STATION, NSTAT), jnp.float32) ** levels(key_of[4], (N_STATION, NSTAT), ((0, 2),), -0.2, 0.2)), 0.2, 5.0)
    return {"features": features, "targets": targets, "station_ids": station_ids, "lead_heads": lead_heads, "station_weight": station_weight}


def factor_heads(gram_sum, moment):
    feat_width = gram_sum.shape[-1]
    identity = jnp.eye(feat_width, dtype=jnp.float32)
    lower_factor = jnp.linalg.cholesky(gram_sum + identity)
    inverse = lax.linalg.triangular_solve(lower_factor, jnp.broadcast_to(identity, gram_sum.shape), left_side=True, lower=True)
    inner_term = jnp.einsum('hkj,hj->hk', inverse, moment, precision=lax.Precision.HIGHEST)
    coefficient = jnp.einsum('hkj,hk->hj', inverse, inner_term, precision=lax.Precision.HIGHEST)
    spreads = jnp.sqrt(lax.optimization_barrier(jnp.sum(inverse * inverse, axis=1)))
    return (inverse, coefficient / spreads)

def reference(features, targets, station_ids, lead_heads, station_weight):
    groups = (jnp.arange(ROWS) // (ROWS // N_STATION)).astype(jnp.int32)
    row_weight = station_weight[groups, station_ids]
    weighted = (row_weight[:, None] * features).astype(jnp.bfloat16)
    block_count = ROWS // BLK
    feat_blocks = features.reshape(block_count, BLK, F)
    weight_blocks = weighted.reshape(block_count, BLK, F)
    target_blocks = targets.reshape(block_count, BLK)
    block_heads = lead_heads.reshape(block_count, BLK)[:, 0]

    def accumulate(totals, block_item):
        gram_sum, moment = totals
        feat_block, weight_block, target_block, head_now = block_item
        gram_sum = gram_sum.at[head_now].add(jnp.dot(weight_block.T.astype(jnp.float32), feat_block.astype(jnp.float32), preferred_element_type=jnp.float32))
        moment = moment.at[head_now].add(jnp.dot(target_block.astype(jnp.float32), weight_block.astype(jnp.float32), preferred_element_type=jnp.float32))
        return ((gram_sum, moment), None)
    start = (jnp.zeros((HEADS, F, F), jnp.float32), jnp.zeros((HEADS, F), jnp.float32))
    (gram_sum, moment), unused = lax.scan(accumulate, start, (feat_blocks, weight_blocks, target_blocks, block_heads))
    inverse, zscores = factor_heads(gram_sum, moment)
    inverse_low = inverse.astype(jnp.bfloat16)

    def block_leverage(block_item):
        feat_block, head_now = block_item
        projected = jnp.dot(feat_block.astype(jnp.float32), inverse_low[head_now].T.astype(jnp.float32), preferred_element_type=jnp.float32)
        return lax.optimization_barrier(jnp.sum(projected * projected, axis=1))
    lev_blocks = lax.map(block_leverage, (feat_blocks, block_heads))
    leverage = row_weight * lev_blocks.reshape(ROWS) * (ROWS / (HEADS * F))
    inverse_factor = inverse * math.sqrt(ROWS / HEADS)
    return (leverage, zscores, inverse_factor)
```

```python
import functools
import math

import jax
import jax.numpy as jnp
from jax import lax
from jax.experimental import pallas as pl
from jax.experimental.pallas import tpu as pltpu
from jax.sharding import PartitionSpec as P

HEADS = 16
BLK = 1024
LANES = 128
SUB = BLK // LANES
HEAD_BITS = 4
F32 = jnp.float32
HIGHEST = lax.Precision.HIGHEST
MESH = pl.DeviceIdType.MESH
PACK_ROWS = 416
VEC_ROW = 384


def bits_of(mesh_shape):
    station, tm = mesh_shape["station"], mesh_shape["tm"]
    core = ("tm", 1)
    owner = [("station", 1), ("tm", 2), ("tm", 4), ("tm", 8)]
    rest = [("station", s) for s in (2**i for i in range(1, 16)) if s < station]
    rest += [("tm", s) for s in (2**i for i in range(4, 16)) if s < tm]
    return core, owner, rest


def bit_value(bit):
    return lax.rem(lax.div(lax.axis_index(bit[0]), bit[1]), 2)


def partner(bit):
    axis, step = bit
    return {axis: lax.axis_index(axis) + (1 - 2 * bit_value(bit)) * step}


def greet(bits):
    barrier = pltpu.get_barrier_semaphore()
    for bit in bits:
        pl.semaphore_signal(barrier, inc=1, device_id=partner(bit), device_id_type=MESH)
    pl.semaphore_wait(barrier, len(bits))


def gram_kernel(heads_ref, feat_ref, ids_ref, tgt_ref, table_ref, out_ref, w_ref, acc, vec, tgt):
    step = pl.program_id(0)

    @pl.when(step == 0)
    def _():
        acc[...] = jnp.zeros_like(acc)
        vec[...] = jnp.zeros_like(vec)
        tgt[...] = tgt_ref[...].astype(F32)

    table = jnp.broadcast_to(table_ref[...], (SUB, LANES))
    weights = jnp.take_along_axis(table, ids_ref[...], axis=1, mode="promise_in_bounds")
    w_ref[...] = weights
    feat = feat_ref[...]
    turned = feat.T
    scaled = jnp.concatenate(
        [
            (turned[:, c * LANES : (c + 1) * LANES].astype(F32) * weights[c : c + 1, :]).astype(
                jnp.bfloat16
            )
            for c in range(SUB)
        ],
        axis=1,
    )
    head = heads_ref[0, 0]
    acc[head] += jnp.dot(scaled, feat, preferred_element_type=F32)
    here = tgt[pl.ds(pl.multiple_of(step * SUB, SUB), SUB), :]
    row = lax.broadcasted_iota(jnp.int32, (SUB, LANES), 0)
    spread = jnp.concatenate([jnp.where(row == c, here, 0.0) for c in range(SUB)], axis=1)
    vec[head] += lax.dot_general(
        spread.astype(jnp.bfloat16), scaled, (((1,), (1,)), ((), ())), preferred_element_type=F32
    )

    @pl.when(step == pl.num_programs(0) - 1)
    def _():
        @pl.loop(0, HEADS)
        def _(h):
            out_ref[h, 0:128, :] = acc[h, 0:128, 0:128]
            out_ref[h, 128:256, :] = 0.5 * (acc[h, 128:256, 0:128] + acc[h, 0:128, 128:256].T)
            out_ref[h, 256:384, :] = acc[h, 128:256, 128:256]
            total = jnp.sum(vec[h], axis=0, keepdims=True)
            out_ref[h, VEC_ROW:PACK_ROWS, :] = jnp.zeros((PACK_ROWS - VEC_ROW, LANES), F32)
            out_ref[h, VEC_ROW : VEC_ROW + 1, :] = total[:, 0:128]
            out_ref[h, VEC_ROW + 1 : VEC_ROW + 2, :] = total[:, 128:256]


def reduce_kernel(plan, g_ref, out_ref, acc, first, fin, *rest):
    core_bit, orders, all_bits = plan
    stage_count = len(orders[0])
    bufs = [rest[c * stage_count : (c + 1) * stage_count] for c in range(2)]
    send, recv = rest[-2:]
    half = PACK_ROWS // 2
    quarter = half // 2
    core = bit_value(core_bit)
    mine = [pl.ds(pl.multiple_of(core * half + c * quarter, 8), quarter) for c in range(2)]
    theirs = [pl.ds(pl.multiple_of((1 - core) * half + c * quarter, 8), quarter) for c in range(2)]
    greet(all_bits)
    sent = []

    def push(src, dst, chain, stage, bit):
        copy = pltpu.make_async_remote_copy(
            src_ref=src,
            dst_ref=dst,
            send_sem=send.at[chain, stage],
            recv_sem=recv.at[chain, stage],
            device_id=partner(bit),
            device_id_type=MESH,
        )
        copy.start()
        sent.append(copy)
        return copy

    flying = [
        push(g_ref.at[:, :, :, :, theirs[c]], first.at[c], c, 0, core_bit) for c in range(2)
    ]
    every = slice(None)
    index = [[every] * HEAD_BITS for _ in range(2)]
    for stage in range(stage_count + 1):
        for c in range(2):
            flying[c].wait_recv()
            if stage == 0:
                acc[c] = g_ref[:, :, :, :, mine[c], :] + first[c]
            else:
                place = (c, *index[c])
                acc[place] = acc[place] + bufs[c][stage - 1][...]
            if stage < stage_count:
                bit, dim = orders[c][stage]
                away = list(index[c])
                if dim is not None:
                    away[dim] = 1 - bit_value(bit)
                    index[c][dim] = bit_value(bit)
                flying[c] = push(acc.at[(c, *away)], bufs[c][stage], c, stage + 1, bit)
            else:
                flying[c] = push(acc.at[(c, *index[c])], fin.at[c], c, stage + 1, core_bit)
    for c in range(2):
        flying[c].wait_recv()
        out_ref[mine[c], :] = acc[(c, *index[c])]
        out_ref[theirs[c], :] = fin[c]
    for copy in sent:
        copy.wait_send()


def gather_kernel(plan, x_ref, out_ref, send, recv, send_core, recv_core):
    core_bit, orders, all_bits = plan
    half = PACK_ROWS // 2
    quarter = half // 2
    core = bit_value(core_bit)
    mine = [pl.ds(pl.multiple_of(core * half + c * quarter, 8), quarter) for c in range(2)]
    own = [None] * HEAD_BITS
    for bit, dim in orders[0]:
        own[dim] = bit_value(bit)
    out_ref[(*own,)] = x_ref[...]
    greet(all_bits)
    sent, late = [], []

    def push(place, chain, bit, send_sem, recv_sem):
        view = out_ref.at[(*place, mine[chain])]
        copy = pltpu.make_async_remote_copy(
            src_ref=view,
            dst_ref=view,
            send_sem=send_sem,
            recv_sem=recv_sem,
            device_id=partner(bit),
            device_id_type=MESH,
        )
        copy.start()
        sent.append(copy)
        return copy

    index = [list(own) for _ in range(2)]
    flying = [None, None]
    for stage in range(HEAD_BITS + 1):
        for c in range(2):
            if stage > 0:
                flying[c].wait_recv()
                bit, dim = orders[c][stage - 1]
                news = list(index[c])
                news[dim] = 1 - bit_value(bit)
                index[c][dim] = slice(None)
            if stage < HEAD_BITS:
                bit, dim = orders[c][stage]
                flying[c] = push(index[c], c, bit, send.at[c, stage], recv.at[c, stage])
            if stage > 0:
                late.append(
                    push(
                        news, c, core_bit, send_core.at[c, stage - 1], recv_core.at[c, stage - 1]
                    )
                )
    for copy in late:
        copy.wait_recv()
    for copy in sent:
        copy.wait_send()


def mm(a, b, dims):
    return lax.dot_general(a, b, (dims, ((), ())), precision=HIGHEST, preferred_element_type=F32)


def eliminate(matrix, offset):
    groups = matrix.shape[0] // 8
    rows = [matrix[8 * g : 8 * g + 8, :] for g in range(groups)]
    below = lax.broadcasted_iota(jnp.int32, (8, LANES), 0)
    for p in range(groups):
        columns = [offset + 8 * p + k for k in range(8)]
        pivots = [None] * 8
        across = [[None] * 8 for _ in range(8)]
        lines = [None] * 8
        for g in range(p, groups):
            cols = [jnp.broadcast_to(rows[g][:, j : j + 1], (8, LANES)) for j in columns]
            for k in range(8):
                if g == p:
                    pivots[k] = 1.0 / cols[k][k : k + 1, :]
                    lines[k] = rows[p][k : k + 1, :]
                    for m in range(k + 1, 8):
                        across[k][m] = cols[m][k : k + 1, :]
                factor = cols[k] * pivots[k]
                if g == p:
                    factor = jnp.where(below > k, factor, 0.0)
                for m in range(k + 1, 8):
                    cols[m] = cols[m] - factor * across[k][m]
                rows[g] = rows[g] - factor * lines[k]
    done = jnp.concatenate(rows, axis=0)
    lane = lax.broadcasted_iota(jnp.int32, done.shape, 1)
    row = lax.broadcasted_iota(jnp.int32, done.shape, 0)
    diagonal = jnp.sum(jnp.where(lane == row + offset, done, 0.0), axis=1, keepdims=True)
    return done * (1.0 / jnp.sqrt(diagonal))


def inverse_factor_128(a):
    lane = lax.broadcasted_iota(jnp.int32, (64, LANES), 1)
    row = lax.broadcasted_iota(jnp.int32, (64, LANES), 0)
    low = lane < 64
    top, bottom = a[0:64, :], a[64:128, :]
    first = eliminate(jnp.where(low, top, (lane == row + 64).astype(F32)), 0)
    x1 = jnp.where(low, pltpu.roll(first, 64, 1), 0.0)
    upper = mm(x1[:, 0:64], top, ((1,), (0,)))
    schur = bottom - mm(upper, upper, ((0,), (0,)))[64:128, :]
    second = eliminate(jnp.where(low, (lane == row).astype(F32), schur), 64)
    x2 = jnp.where(low, second, 0.0)
    across = mm(upper, x1, ((0,), (0,)))[64:128, :]
    x21 = -mm(x2[:, 0:64], across, ((1,), (0,)))
    return jnp.concatenate([x1, x21 + pltpu.roll(x2, 64, 1)], axis=0)


def factor_kernel(g_ref, out_ref):
    size = LANES
    eye = (
        lax.broadcasted_iota(jnp.int32, (size, size), 0)
        == lax.broadcasted_iota(jnp.int32, (size, size), 1)
    ).astype(F32)
    g11 = g_ref[0:128, :]
    g21 = g_ref[128:256, :]
    g22 = g_ref[256:384, :]
    x1 = inverse_factor_128(0.5 * (g11 + g11.T) + eye)
    out_ref[0:128, :] = x1
    lower = mm(g21, x1, ((1,), (1,)))
    x2 = inverse_factor_128(0.5 * (g22 + g22.T) + eye - mm(lower, lower, ((1,), (1,))))
    out_ref[256:384, :] = x2
    x21 = -mm(x2, mm(lower, x1, ((1,), (0,))), ((1,), (0,)))
    out_ref[128:256, :] = x21
    m1 = jnp.broadcast_to(g_ref[VEC_ROW : VEC_ROW + 1, :], (8, LANES))
    m2 = jnp.broadcast_to(g_ref[VEC_ROW + 1 : VEC_ROW + 2, :], (8, LANES))
    in1 = mm(m1, x1, ((1,), (1,)))
    in2 = mm(m1, x21, ((1,), (1,))) + mm(m2, x2, ((1,), (1,)))
    co1 = mm(in1, x1, ((1,), (0,))) + mm(in2, x21, ((1,), (0,)))
    co2 = mm(in2, x2, ((1,), (0,)))
    s1 = jnp.sum(x1 * x1, axis=0, keepdims=True) + jnp.sum(x21 * x21, axis=0, keepdims=True)
    s2 = jnp.sum(x2 * x2, axis=0, keepdims=True)
    out_ref[VEC_ROW:PACK_ROWS, :] = jnp.zeros((PACK_ROWS - VEC_ROW, LANES), F32)
    out_ref[VEC_ROW : VEC_ROW + 1, :] = co1[0:1, :] / jnp.sqrt(s1)
    out_ref[VEC_ROW + 1 : VEC_ROW + 2, :] = co2[0:1, :] / jnp.sqrt(s2)


def leverage_kernel(scale, place_ref, heads_ref, feat_ref, w_ref, inv_ref, lev_ref, z_ref, piece_ref):
    step = pl.program_id(0)

    @pl.when(step == 0)
    def _():
        z_ref[:, 0:128] = inv_ref[:, VEC_ROW, :]
        z_ref[:, 128:256] = inv_ref[:, VEC_ROW + 1, :]
        count = piece_ref.shape[1]
        start = place_ref[0] * count
        root = math.sqrt(scale * 2 * LANES)
        left = inv_ref[:, pl.ds(pl.multiple_of(start, 8), count), :]
        spot = pl.multiple_of(jnp.maximum(start - 128, 0) + 256, 8)
        right = inv_ref[:, pl.ds(spot, count), :]
        piece_ref[:, :, 0:128] = left * root
        piece_ref[:, :, 128:256] = jnp.where(start >= 128, right * root, 0.0)

    head = heads_ref[0, 0]
    zero = jnp.zeros((128, 128), jnp.bfloat16)
    x1 = inv_ref[head, 0:128, :].astype(jnp.bfloat16)
    x21 = inv_ref[head, 128:256, :].astype(jnp.bfloat16)
    x2 = inv_ref[head, 256:384, :].astype(jnp.bfloat16)
    low = jnp.concatenate(
        [jnp.concatenate([x1, zero], axis=1), jnp.concatenate([x21, x2], axis=1)], axis=0
    )
    turned = lax.dot_general(
        low, feat_ref[...], (((1,), (1,)), ((), ())), preferred_element_type=F32
    )
    squares = jnp.sum(turned * turned, axis=0, keepdims=True)
    for c in range(SUB):
        lev_ref[c : c + 1, :] = w_ref[c : c + 1, :] * squares[:, c * LANES : (c + 1) * LANES] * scale


def local(mesh_shape, features, targets, station_ids, lead_heads, station_weight):
    row_count, width = features.shape
    blocks = row_count // BLK
    lines = row_count // LANES
    tm = mesh_shape["tm"]
    total_rows = row_count * mesh_shape["station"] * tm
    scale = total_rows / (HEADS * width)
    ids = station_ids.reshape(lines, LANES)
    heads = lead_heads.reshape(lines, LANES)
    goals = targets.reshape(lines, LANES)
    head_spec = pl.BlockSpec((SUB, LANES), lambda b: (b, 0), memory_space=pltpu.SMEM)
    line_spec = pl.BlockSpec((SUB, LANES), lambda b: (b, 0))
    feat_spec = pl.BlockSpec((BLK, width), lambda b: (b, 0))
    big = 48 * 1024 * 1024
    packed, weights = pl.pallas_call(
        gram_kernel,
        grid=(blocks,),
        in_specs=[
            head_spec,
            feat_spec,
            line_spec,
            pl.BlockSpec((lines, LANES), lambda b: (0, 0)),
            pl.BlockSpec((1, LANES), lambda b: (0, 0)),
        ],
        out_specs=[pl.BlockSpec((HEADS, PACK_ROWS, LANES), lambda b: (0, 0, 0)), line_spec],
        out_shape=[
            jax.ShapeDtypeStruct((HEADS, PACK_ROWS, LANES), F32),
            jax.ShapeDtypeStruct((lines, LANES), F32),
        ],
        scratch_shapes=[
            pltpu.VMEM((HEADS, width, width), F32),
            pltpu.VMEM((HEADS, 8, width), F32),
            pltpu.VMEM((lines, LANES), F32),
        ],
        compiler_params=pltpu.CompilerParams(vmem_limit_bytes=big),
        name="gram",
    )(heads, features, ids, goals, station_weight)

    core_bit, owner, rest = bits_of(mesh_shape)
    named = [(bit, dim) for dim, bit in enumerate(owner)]
    x, y, z0, z1 = named
    tail = [(bit, None) for bit in rest]
    down = ([x, y, z0, z1] + tail, [y, x, z0, z1] + tail)
    up = ([z1, z0, y, x], [z1, z0, x, y])
    dims = (2,) * HEAD_BITS
    quarter = PACK_ROWS // 4
    buffers = []
    for c in range(2):
        free = HEAD_BITS
        for bit, dim in down[c]:
            free -= dim is not None
            buffers.append(pltpu.VMEM((2,) * free + (quarter, LANES), F32))
    vmem = pl.BlockSpec(memory_space=pltpu.VMEM)
    summed = pl.pallas_call(
        functools.partial(reduce_kernel, (core_bit, down, [core_bit] + owner + rest)),
        out_shape=jax.ShapeDtypeStruct((PACK_ROWS, LANES), F32),
        in_specs=[vmem],
        out_specs=vmem,
        scratch_shapes=[
            pltpu.VMEM((2, *dims, quarter, LANES), F32),
            pltpu.VMEM((2, *dims, quarter, LANES), F32),
            pltpu.VMEM((2, quarter, LANES), F32),
            *buffers,
            pltpu.SemaphoreType.DMA((2, len(down[0]) + 2)),
            pltpu.SemaphoreType.DMA((2, len(down[0]) + 2)),
        ],
        compiler_params=pltpu.CompilerParams(
            collective_id=0, has_side_effects=True, vmem_limit_bytes=big
        ),
        name="reduce",
    )(packed.reshape(*dims, PACK_ROWS, LANES))

    solved = pl.pallas_call(
        factor_kernel,
        out_shape=jax.ShapeDtypeStruct((PACK_ROWS, LANES), F32),
        in_specs=[vmem],
        out_specs=vmem,
        compiler_params=pltpu.CompilerParams(vmem_limit_bytes=big),
        name="factor",
    )(summed)

    everyone = pl.pallas_call(
        functools.partial(gather_kernel, (core_bit, up, [core_bit] + owner)),
        out_shape=jax.ShapeDtypeStruct((*dims, PACK_ROWS, LANES), F32),
        in_specs=[vmem],
        out_specs=vmem,
        scratch_shapes=[
            pltpu.SemaphoreType.DMA((2, HEAD_BITS)),
            pltpu.SemaphoreType.DMA((2, HEAD_BITS)),
            pltpu.SemaphoreType.DMA((2, HEAD_BITS)),
            pltpu.SemaphoreType.DMA((2, HEAD_BITS)),
        ],
        compiler_params=pltpu.CompilerParams(
            collective_id=1, has_side_effects=True, vmem_limit_bytes=big
        ),
        name="gather",
    )(solved).reshape(HEADS, PACK_ROWS, LANES)

    piece_rows = width // tm
    place = lax.axis_index("tm").reshape(1).astype(jnp.int32)
    leverage, zscores, pieces = pl.pallas_call(
        functools.partial(leverage_kernel, scale),
        grid=(blocks,),
        in_specs=[
            pl.BlockSpec(memory_space=pltpu.SMEM),
            head_spec,
            feat_spec,
            line_spec,
            pl.BlockSpec((HEADS, PACK_ROWS, LANES), lambda b: (0, 0, 0)),
        ],
        out_specs=[
            line_spec,
            pl.BlockSpec((HEADS, width), lambda b: (0, 0)),
            pl.BlockSpec((HEADS, piece_rows, width), lambda b: (0, 0, 0)),
        ],
        out_shape=[
            jax.ShapeDtypeStruct((lines, LANES), F32),
            jax.ShapeDtypeStruct((HEADS, width), F32),
            jax.ShapeDtypeStruct((HEADS, piece_rows, width), F32),
        ],
        compiler_params=pltpu.CompilerParams(vmem_limit_bytes=big),
        name="leverage",
    )(place, heads, features, weights, everyone)
    return (leverage.reshape(row_count), zscores, pieces)


def solution(mesh):
    return jax.shard_map(
        functools.partial(local, dict(mesh.shape)),
        mesh=mesh,
        in_specs=(
            P(("station", "tm"), None),
            P(("station", "tm")),
            P(("station", "tm")),
            P(("station", "tm")),
            P("station", None),
        ),
        out_specs=(P(("station", "tm")), P(), P(None, "tm", None)),
        check_vma=False,
    )
```

```python
import functools
import math

import jax
import jax.numpy as jnp
from jax import lax
from jax.experimental import pallas as pl
from jax.experimental.pallas import tpu as pltpu
from jax.sharding import PartitionSpec as P

HEADS = 16
BLK = 1024
LANES = 128
SUB = BLK // LANES
HEAD_BITS = 4
F32 = jnp.float32
HIGHEST = lax.Precision.HIGHEST
MESH = pl.DeviceIdType.MESH
PACK_ROWS = 336
VEC_ROW = 320
CHAINS = ((0, 48), (48, 40), (88, 40), (128, 40))


def bits_of(mesh_shape):
    station, tm = mesh_shape["station"], mesh_shape["tm"]
    core = ("tm", 1)
    owner = [("station", 1), ("tm", 2), ("tm", 4), ("tm", 8)]
    rest = [("station", s) for s in (2**i for i in range(1, 16)) if s < station]
    rest += [("tm", s) for s in (2**i for i in range(4, 16)) if s < tm]
    return core, owner, rest


def bit_value(bit):
    return lax.rem(lax.div(lax.axis_index(bit[0]), bit[1]), 2)


def partner(bit):
    axis, step = bit
    return {axis: lax.axis_index(axis) + (1 - 2 * bit_value(bit)) * step}


def greet(bits):
    barrier = pltpu.get_barrier_semaphore()
    for bit in bits:
        pl.semaphore_signal(barrier, inc=1, device_id=partner(bit), device_id_type=MESH)
    pl.semaphore_wait(barrier, len(bits))


def half_tiles(full):
    return full[64:128, :], full[0:64, :]


def gram_kernel(
    heads_hbm, feat_ref, ids_hbm, tgt_hbm, table_hbm, out_ref, w_ref, acc, vec, heads, ids, low, tgt, table, sems
):
    step = pl.program_id(0)
    per = feat_ref.shape[0] // BLK

    @pl.when(step == 0)
    def _():
        copies = [
            pltpu.make_async_copy(src, dst, sems.at[i])
            for i, (src, dst) in enumerate(
                ((ids_hbm, ids), (table_hbm, table), (tgt_hbm, low), (heads_hbm, heads))
            )
        ]
        for copy in copies:
            copy.start()
        acc[...] = jnp.zeros_like(acc)
        vec[...] = jnp.zeros_like(vec)
        for copy in copies:
            copy.wait()
        tgt[...] = low[...].astype(F32)

    lookup = jnp.broadcast_to(table[...], (SUB, LANES))
    row = lax.broadcasted_iota(jnp.int32, (SUB, LANES), 0)
    for i in range(per):
        line = pl.multiple_of((step * per + i) * SUB, SUB)
        weights = jnp.take_along_axis(
            lookup, ids[pl.ds(line, SUB), :], axis=1, mode="promise_in_bounds"
        )
        w_ref[i * SUB : (i + 1) * SUB, :] = weights
        feat = feat_ref[i * BLK : (i + 1) * BLK, :]
        turned = feat.T
        scaled = jnp.concatenate(
            [
                (turned[:, c * LANES : (c + 1) * LANES].astype(F32) * weights[c : c + 1, :]).astype(
                    jnp.bfloat16
                )
                for c in range(SUB)
            ],
            axis=1,
        )
        head = heads[line, 0]
        acc[head] += jnp.dot(scaled, feat, preferred_element_type=F32)
        here = tgt[pl.ds(line, SUB), :]
        spread = jnp.concatenate([jnp.where(row == c, here, 0.0) for c in range(SUB)], axis=1)
        vec[head] += lax.dot_general(
            spread.astype(jnp.bfloat16),
            scaled,
            (((1,), (1,)), ((), ())),
            preferred_element_type=F32,
        )

    @pl.when(step == pl.num_programs(0) - 1)
    def _():
        left = lax.broadcasted_iota(jnp.int32, (64, LANES), 1) < 64

        @pl.loop(0, HEADS)
        def _(h):
            g11, g22 = acc[h, 0:128, 0:128], acc[h, 128:256, 128:256]
            lower1, top1 = half_tiles(0.5 * (g11 + g11.T))
            lower2, top2 = half_tiles(0.5 * (g22 + g22.T))
            out_ref[h, 0:64, :] = jnp.where(left, top1, pltpu.roll(top2, 64, 1))
            out_ref[h, 64:128, :] = lower1
            out_ref[h, 128:192, :] = lower2
            out_ref[h, 192:320, :] = 0.5 * (acc[h, 128:256, 0:128] + acc[h, 0:128, 128:256].T)
            total = jnp.sum(vec[h], axis=0, keepdims=True)
            out_ref[h, VEC_ROW:PACK_ROWS, :] = jnp.zeros((PACK_ROWS - VEC_ROW, LANES), F32)
            out_ref[h, VEC_ROW : VEC_ROW + 1, :] = total[:, 0:128]
            out_ref[h, VEC_ROW + 1 : VEC_ROW + 2, :] = total[:, 128:256]


def reduce_kernel(plan, g_ref, out_ref, acc, first, fin, *rest):
    core_bit, orders, all_bits = plan
    stage_count = len(orders[0])
    count = len(CHAINS)
    bufs = [rest[c * stage_count : (c + 1) * stage_count] for c in range(count)]
    send, recv = rest[-2:]
    half = PACK_ROWS // 2
    core = bit_value(core_bit)
    own = [pl.ds(start, size) for start, size in CHAINS]
    mine = [pl.ds(pl.multiple_of(core * half + start, 8), size) for start, size in CHAINS]
    theirs = [pl.ds(pl.multiple_of((1 - core) * half + start, 8), size) for start, size in CHAINS]
    greet(all_bits)
    sent = []
    flying = [None] * count
    index = [[slice(None)] * HEAD_BITS for _ in range(count)]

    def push(src, dst, chain, stage, bit):
        copy = pltpu.make_async_remote_copy(
            src_ref=src,
            dst_ref=dst,
            send_sem=send.at[chain, stage],
            recv_sem=recv.at[chain, stage],
            device_id=partner(bit),
            device_id_type=MESH,
        )
        copy.start()
        sent.append(copy)
        flying[chain] = copy

    def take(c, stage):
        flying[c].wait_recv()
        place = (*index[c], own[c])
        if stage == 0:
            acc[place] = g_ref[:, :, :, :, mine[c], :] + first[place]
        else:
            acc[place] = acc[place] + bufs[c][stage - 1][...]

    def give(c, stage):
        if stage == stage_count:
            push(acc.at[(*index[c], own[c])], fin.at[own[c]], c, stage + 1, core_bit)
            return
        bit, dim = orders[c % 2][stage]
        away = list(index[c])
        if dim is not None:
            away[dim] = 1 - bit_value(bit)
            index[c][dim] = bit_value(bit)
        push(acc.at[(*away, own[c])], bufs[c][stage], c, stage + 1, bit)

    every = [slice(None)] * HEAD_BITS
    for c in range(count):
        push(g_ref.at[(*every, theirs[c])], first.at[(*every, own[c])], c, 0, core_bit)
    ahead, behind = (0, 1), (2, 3)
    for c in ahead:
        take(c, 0)
        give(c, 0)
    for c in behind:
        take(c, 0)
    for stage in range(1, stage_count + 1):
        for c in ahead:
            take(c, stage)
            give(c, stage)
        for c in behind:
            if stage > 1:
                take(c, stage - 1)
            give(c, stage - 1)
    for c in behind:
        take(c, stage_count)
        give(c, stage_count)
    for c in range(count):
        flying[c].wait_recv()
        out_ref[mine[c], :] = acc[(*index[c], own[c])]
        out_ref[theirs[c], :] = fin[own[c], :]
    for copy in sent:
        copy.wait_send()


def gather_kernel(plan, x_ref, out_ref, send, recv, send_core, recv_core):
    core_bit, orders, all_bits = plan
    count = len(CHAINS)
    half = PACK_ROWS // 2
    core = bit_value(core_bit)
    mine = [pl.ds(pl.multiple_of(core * half + start, 8), size) for start, size in CHAINS]
    own = [None] * HEAD_BITS
    for bit, dim in orders[0]:
        own[dim] = bit_value(bit)
    out_ref[(*own,)] = x_ref[...]
    greet(all_bits)
    sent, late = [], []

    def push(place, chain, bit, send_sem, recv_sem):
        view = out_ref.at[(*place, mine[chain])]
        copy = pltpu.make_async_remote_copy(
            src_ref=view,
            dst_ref=view,
            send_sem=send_sem,
            recv_sem=recv_sem,
            device_id=partner(bit),
            device_id_type=MESH,
        )
        copy.start()
        sent.append(copy)
        return copy

    index = [list(own) for _ in range(count)]
    flying = [None] * count

    def give(c, stage):
        if stage < HEAD_BITS:
            bit, dim = orders[c % 2][stage]
            flying[c] = push(index[c], c, bit, send.at[c, stage], recv.at[c, stage])

    def take(c, stage):
        flying[c].wait_recv()
        bit, dim = orders[c % 2][stage]
        news = list(index[c])
        news[dim] = 1 - bit_value(bit)
        index[c][dim] = slice(None)
        give(c, stage + 1)
        late.append(push(news, c, core_bit, send_core.at[c, stage], recv_core.at[c, stage]))

    ahead, behind = (0, 1), (2, 3)
    for c in ahead:
        give(c, 0)
    for stage in range(HEAD_BITS + 2):
        for c in ahead:
            if stage < HEAD_BITS:
                take(c, stage)
        for c in behind:
            if stage == 1:
                give(c, 0)
            if stage >= 2:
                take(c, stage - 2)
    for copy in late:
        copy.wait_recv()
    for copy in sent:
        copy.wait_send()


def mm(a, b, dims):
    return lax.dot_general(a, b, (dims, ((), ())), precision=HIGHEST, preferred_element_type=F32)


def eliminate(matrix, offset):
    groups = matrix.shape[0] // 8
    rows = [matrix[8 * g : 8 * g + 8, :] for g in range(groups)]
    below = lax.broadcasted_iota(jnp.int32, (8, LANES), 0)
    for p in range(groups):
        columns = [offset + 8 * p + k for k in range(8)]
        pivots = [None] * 8
        across = [[None] * 8 for _ in range(8)]
        lines = [None] * 8
        for g in range(p, groups):
            cols = [jnp.broadcast_to(rows[g][:, j : j + 1], (8, LANES)) for j in columns]
            for k in range(8):
                if g == p:
                    pivots[k] = 1.0 / cols[k][k : k + 1, :]
                    lines[k] = rows[p][k : k + 1, :]
                    for m in range(k + 1, 8):
                        across[k][m] = cols[m][k : k + 1, :]
                factor = cols[k] * pivots[k]
                if g == p:
                    factor = jnp.where(below > k, factor, 0.0)
                for m in range(k + 1, 8):
                    cols[m] = cols[m] - factor * across[k][m]
                rows[g] = rows[g] - factor * lines[k]
    done = jnp.concatenate(rows, axis=0)
    lane = lax.broadcasted_iota(jnp.int32, done.shape, 1)
    row = lax.broadcasted_iota(jnp.int32, done.shape, 0)
    diagonal = jnp.sum(jnp.where(lane == row + offset, done, 0.0), axis=1, keepdims=True)
    return done * (1.0 / jnp.sqrt(diagonal))


def inverse_factor_128(top, bottom):
    lane = lax.broadcasted_iota(jnp.int32, (64, LANES), 1)
    row = lax.broadcasted_iota(jnp.int32, (64, LANES), 0)
    low = lane < 64
    eye = (lane == row + 64).astype(F32)
    none = jnp.zeros((64, LANES), F32)
    first = eliminate(jnp.where(low, top, eye), 0)
    x1 = jnp.where(low, pltpu.roll(first, 64, 1), 0.0)
    x1_full = jnp.concatenate([x1, none], axis=0)
    lower = mm(bottom, x1_full, ((1,), (1,)))
    square = mm(lower, jnp.concatenate([lower, none], axis=0), ((1,), (1,)))
    second = eliminate(jnp.where(low, pltpu.roll(bottom, 64, 1) - square, eye), 0)
    x2 = jnp.where(low, 0.0, second)
    across = mm(lower, x1_full, ((1,), (0,)))
    x21 = -mm(x2, jnp.concatenate([none, across], axis=0), ((1,), (0,)))
    return x1, x21 + x2


def factor_kernel(g_ref, out_ref):
    lane = lax.broadcasted_iota(jnp.int32, (64, LANES), 1)
    row = lax.broadcasted_iota(jnp.int32, (64, LANES), 0)
    low = lane < 64
    eye_top = (lane == row).astype(F32)
    eye_bottom = (lane == row + 64).astype(F32)
    tops = g_ref[0:64, :]
    top1, bottom1 = inverse_factor_128(tops + eye_top, g_ref[64:128, :] + eye_bottom)
    x1 = jnp.concatenate([top1, bottom1], axis=0)
    lower = mm(g_ref[192:320, :], x1, ((1,), (1,)))
    square = mm(lower, lower, ((1,), (1,)))
    top2, bottom2 = inverse_factor_128(
        pltpu.roll(tops, 64, 1) + eye_top - square[0:64, :],
        g_ref[128:192, :] + eye_bottom - square[64:128, :],
    )
    x2 = jnp.concatenate([top2, bottom2], axis=0)
    x21 = -mm(x2, mm(lower, x1, ((1,), (0,))), ((1,), (0,)))
    out_ref[0:64, :] = jnp.where(low, top1, pltpu.roll(top2, 64, 1))
    out_ref[64:128, :] = bottom1
    out_ref[128:192, :] = bottom2
    out_ref[192:320, :] = x21
    m1 = jnp.broadcast_to(g_ref[VEC_ROW : VEC_ROW + 1, :], (8, LANES))
    m2 = jnp.broadcast_to(g_ref[VEC_ROW + 1 : VEC_ROW + 2, :], (8, LANES))
    in1 = mm(m1, x1, ((1,), (1,)))
    in2 = mm(m1, x21, ((1,), (1,))) + mm(m2, x2, ((1,), (1,)))
    co1 = mm(in1, x1, ((1,), (0,))) + mm(in2, x21, ((1,), (0,)))
    co2 = mm(in2, x2, ((1,), (0,)))
    s1 = jnp.sum(x1 * x1, axis=0, keepdims=True) + jnp.sum(x21 * x21, axis=0, keepdims=True)
    s2 = jnp.sum(x2 * x2, axis=0, keepdims=True)
    out_ref[VEC_ROW:PACK_ROWS, :] = jnp.zeros((PACK_ROWS - VEC_ROW, LANES), F32)
    out_ref[VEC_ROW : VEC_ROW + 1, :] = co1[0:1, :] / jnp.sqrt(s1)
    out_ref[VEC_ROW + 1 : VEC_ROW + 2, :] = co2[0:1, :] / jnp.sqrt(s2)


def leverage_kernel(scale, place_ref, heads_ref, feat_ref, w_ref, inv_ref, lev_ref, z_ref, piece_ref):
    step = pl.program_id(0)
    per = feat_ref.shape[0] // BLK

    @pl.when(step == 0)
    def _():
        z_ref[:, 0:128] = inv_ref[:, VEC_ROW, :]
        z_ref[:, 128:256] = inv_ref[:, VEC_ROW + 1, :]
        count = piece_ref.shape[1]
        start = place_ref[0] * count
        root = math.sqrt(scale * 2 * LANES)
        low = lax.broadcasted_iota(jnp.int32, (count, LANES), 1) < 64

        def rows(first):
            return inv_ref[:, pl.ds(pl.multiple_of(first, 8), count), :] * root

        @pl.when(start < 64)
        def _():
            piece_ref[:, :, 0:128] = jnp.where(low, rows(start), 0.0)

        @pl.when(jnp.logical_and(start >= 64, start < 128))
        def _():
            piece_ref[:, :, 0:128] = rows(start)

        @pl.when(start < 128)
        def _():
            piece_ref[:, :, 128:256] = jnp.zeros((HEADS, count, LANES), F32)

        @pl.when(start >= 128)
        def _():
            piece_ref[:, :, 0:128] = rows(start + 64)

        @pl.when(jnp.logical_and(start >= 128, start < 192))
        def _():
            for h in range(HEADS):
                part = inv_ref[h, pl.ds(pl.multiple_of(start - 128, 8), count), :] * root
                piece_ref[h, :, 128:256] = jnp.where(low, pltpu.roll(part, 64, 1), 0.0)

        @pl.when(start >= 192)
        def _():
            piece_ref[:, :, 128:256] = rows(start - 64)

    low = lax.broadcasted_iota(jnp.int32, (64, LANES), 1) < 64
    zero = jnp.zeros((128, 128), jnp.bfloat16)
    for i in range(per):
        head = heads_ref[i * SUB, 0]
        tops = inv_ref[head, 0:64, :]
        x1 = jnp.concatenate([jnp.where(low, tops, 0.0), inv_ref[head, 64:128, :]], axis=0)
        x2 = jnp.concatenate(
            [jnp.where(low, pltpu.roll(tops, 64, 1), 0.0), inv_ref[head, 128:192, :]], axis=0
        )
        x21 = inv_ref[head, 192:320, :]
        x1, x21, x2 = (x.astype(jnp.bfloat16) for x in (x1, x21, x2))
        inverse = jnp.concatenate(
            [jnp.concatenate([x1, zero], axis=1), jnp.concatenate([x21, x2], axis=1)], axis=0
        )
        projected = lax.dot_general(
            feat_ref[i * BLK : (i + 1) * BLK, :],
            inverse,
            (((1,), (1,)), ((), ())),
            preferred_element_type=F32,
        )
        one, two = projected[:, 0:128], projected[:, 128:256]
        squares = one * one + two * two
        for c in range(SUB):
            line = jnp.sum(squares[c * LANES : (c + 1) * LANES, :].T, axis=0, keepdims=True)
            here = i * SUB + c
            lev_ref[here : here + 1, :] = w_ref[here : here + 1, :] * line * scale


def local(mesh_shape, features, targets, station_ids, lead_heads, station_weight):
    row_count, width = features.shape
    blocks = row_count // BLK
    lines = row_count // LANES
    tm = mesh_shape["tm"]
    total_rows = row_count * mesh_shape["station"] * tm
    scale = total_rows / (HEADS * width)
    ids = station_ids.reshape(lines, LANES)
    heads = lead_heads.reshape(lines, LANES)
    goals = targets.reshape(lines, LANES)
    per = math.gcd(blocks, 4)
    head_spec = pl.BlockSpec((per * SUB, LANES), lambda b: (b, 0), memory_space=pltpu.SMEM)
    line_spec = pl.BlockSpec((per * SUB, LANES), lambda b: (b, 0))
    feat_spec = pl.BlockSpec((per * BLK, width), lambda b: (b, 0))
    away = pl.BlockSpec(memory_space=pltpu.HBM)
    big = 48 * 1024 * 1024
    packed, weights = pl.pallas_call(
        gram_kernel,
        grid=(blocks // per,),
        in_specs=[
            away,
            feat_spec,
            away,
            away,
            away,
        ],
        out_specs=[pl.BlockSpec((HEADS, PACK_ROWS, LANES), lambda b: (0, 0, 0)), line_spec],
        out_shape=[
            jax.ShapeDtypeStruct((HEADS, PACK_ROWS, LANES), F32),
            jax.ShapeDtypeStruct((lines, LANES), F32),
        ],
        scratch_shapes=[
            pltpu.VMEM((HEADS, width, width), F32),
            pltpu.VMEM((HEADS, 8, width), F32),
            pltpu.SMEM((lines, LANES), jnp.int32),
            pltpu.VMEM((lines, LANES), jnp.int32),
            pltpu.VMEM((lines, LANES), jnp.bfloat16),
            pltpu.VMEM((lines, LANES), F32),
            pltpu.VMEM(station_weight.shape, F32),
            pltpu.SemaphoreType.DMA((4,)),
        ],
        compiler_params=pltpu.CompilerParams(vmem_limit_bytes=big),
        name="gram",
    )(heads, features, ids, goals, station_weight)

    core_bit, owner, rest = bits_of(mesh_shape)
    named = [(bit, dim) for dim, bit in enumerate(owner)]
    x, y, z0, z1 = named
    tail = [(bit, None) for bit in rest]
    down = ([x, y, z0, z1] + tail, [y, x, z0, z1] + tail)
    up = ([z1, z0, y, x], [z1, z0, x, y])
    dims = (2,) * HEAD_BITS
    half = PACK_ROWS // 2
    count = len(CHAINS)
    buffers = []
    for c, (_, size) in enumerate(CHAINS):
        free = HEAD_BITS
        for bit, dim in down[c % 2]:
            free -= dim is not None
            buffers.append(pltpu.VMEM((2,) * free + (size, LANES), F32))
    vmem = pl.BlockSpec(memory_space=pltpu.VMEM)
    summed = pl.pallas_call(
        functools.partial(reduce_kernel, (core_bit, down, [core_bit] + owner + rest)),
        out_shape=jax.ShapeDtypeStruct((PACK_ROWS, LANES), F32),
        in_specs=[vmem],
        out_specs=vmem,
        scratch_shapes=[
            pltpu.VMEM((*dims, half, LANES), F32),
            pltpu.VMEM((*dims, half, LANES), F32),
            pltpu.VMEM((half, LANES), F32),
            *buffers,
            pltpu.SemaphoreType.DMA((count, len(down[0]) + 2)),
            pltpu.SemaphoreType.DMA((count, len(down[0]) + 2)),
        ],
        compiler_params=pltpu.CompilerParams(
            collective_id=0, has_side_effects=True, vmem_limit_bytes=big
        ),
        name="reduce",
    )(packed.reshape(*dims, PACK_ROWS, LANES))

    solved = pl.pallas_call(
        factor_kernel,
        out_shape=jax.ShapeDtypeStruct((PACK_ROWS, LANES), F32),
        in_specs=[vmem],
        out_specs=vmem,
        compiler_params=pltpu.CompilerParams(vmem_limit_bytes=big),
        name="factor",
    )(summed)

    everyone = pl.pallas_call(
        functools.partial(gather_kernel, (core_bit, up, [core_bit] + owner)),
        out_shape=jax.ShapeDtypeStruct((*dims, PACK_ROWS, LANES), F32),
        in_specs=[vmem],
        out_specs=vmem,
        scratch_shapes=[
            pltpu.SemaphoreType.DMA((count, HEAD_BITS)),
            pltpu.SemaphoreType.DMA((count, HEAD_BITS)),
            pltpu.SemaphoreType.DMA((count, HEAD_BITS)),
            pltpu.SemaphoreType.DMA((count, HEAD_BITS)),
        ],
        compiler_params=pltpu.CompilerParams(
            collective_id=1, has_side_effects=True, vmem_limit_bytes=big
        ),
        name="gather",
    )(solved).reshape(HEADS, PACK_ROWS, LANES)

    piece_rows = width // tm
    place = lax.axis_index("tm").reshape(1).astype(jnp.int32)
    leverage, zscores, pieces = pl.pallas_call(
        functools.partial(leverage_kernel, scale),
        grid=(blocks // per,),
        in_specs=[
            pl.BlockSpec(memory_space=pltpu.SMEM),
            head_spec,
            feat_spec,
            line_spec,
            pl.BlockSpec((HEADS, PACK_ROWS, LANES), lambda b: (0, 0, 0)),
        ],
        out_specs=[
            line_spec,
            pl.BlockSpec((HEADS, width), lambda b: (0, 0)),
            pl.BlockSpec((HEADS, piece_rows, width), lambda b: (0, 0, 0)),
        ],
        out_shape=[
            jax.ShapeDtypeStruct((lines, LANES), F32),
            jax.ShapeDtypeStruct((HEADS, width), F32),
            jax.ShapeDtypeStruct((HEADS, piece_rows, width), F32),
        ],
        compiler_params=pltpu.CompilerParams(vmem_limit_bytes=big),
        name="leverage",
    )(place, heads, features, weights, everyone)
    return (leverage.reshape(row_count), zscores, pieces)


def solution(mesh):
    return jax.shard_map(
        functools.partial(local, dict(mesh.shape)),
        mesh=mesh,
        in_specs=(
            P(("station", "tm"), None),
            P(("station", "tm")),
            P(("station", "tm")),
            P(("station", "tm")),
            P("station", None),
        ),
        out_specs=(P(("station", "tm")), P(), P(None, "tm", None)),
        check_vma=False,
    )
```

```python
import functools
import math

import jax
import jax.numpy as jnp
from jax import lax
from jax.experimental import pallas as pl
from jax.experimental.pallas import tpu as pltpu
from jax.sharding import PartitionSpec as P

HEADS = 16
BLK = 1024
LANES = 128
SUB = BLK // LANES
HEAD_BITS = 4
F32 = jnp.float32
HIGHEST = lax.Precision.HIGHEST
MESH = pl.DeviceIdType.MESH
PACK_ROWS = 336
VEC_ROW = 320
CHAINS = ((0, 32), (32, 32), (64, 56), (120, 48))


def bits_of(mesh_shape):
    station, tm = mesh_shape["station"], mesh_shape["tm"]
    core = ("tm", 1)
    owner = [("station", 1), ("tm", 2), ("tm", 4), ("tm", 8)]
    rest = [("station", s) for s in (2**i for i in range(1, 16)) if s < station]
    rest += [("tm", s) for s in (2**i for i in range(4, 16)) if s < tm]
    return core, owner, rest


def bit_value(bit):
    return lax.rem(lax.div(lax.axis_index(bit[0]), bit[1]), 2)


def moves_of(bits):
    return range(1, 2 ** len(bits))


def partner(bits, move):
    place = {}
    for i, (axis, step) in enumerate(bits):
        if (move >> i) & 1:
            here = place.get(axis, lax.axis_index(axis))
            place[axis] = here + (1 - 2 * bit_value((axis, step))) * step
    return place


def flipped(bit, i, move):
    value = bit_value(bit)
    return 1 - value if (move >> i) & 1 else value


def greet(groups):
    barrier = pltpu.get_barrier_semaphore()
    met = 0
    for bits in groups:
        for move in moves_of(bits):
            pl.semaphore_signal(
                barrier, inc=1, device_id=partner(bits, move), device_id_type=MESH
            )
            met += 1
    pl.semaphore_wait(barrier, met)


def half_tiles(full):
    return full[64:128, :], full[0:64, :]


def gram_kernel(
    heads_hbm, feat_ref, ids_hbm, tgt_hbm, table_hbm, out_ref, w_ref, acc, vec, heads, ids, low, tgt, table, sems
):
    step = pl.program_id(0)
    per = feat_ref.shape[0] // BLK

    @pl.when(step == 0)
    def _():
        copies = [
            pltpu.make_async_copy(src, dst, sems.at[i])
            for i, (src, dst) in enumerate(
                ((ids_hbm, ids), (table_hbm, table), (tgt_hbm, low), (heads_hbm, heads))
            )
        ]
        for copy in copies:
            copy.start()
        acc[...] = jnp.zeros_like(acc)
        vec[...] = jnp.zeros_like(vec)
        for copy in copies:
            copy.wait()
        tgt[...] = low[...].astype(F32)

    lookup = jnp.broadcast_to(table[...], (SUB, LANES))
    row = lax.broadcasted_iota(jnp.int32, (SUB, LANES), 0)
    for i in range(per):
        line = pl.multiple_of((step * per + i) * SUB, SUB)
        weights = jnp.take_along_axis(
            lookup, ids[pl.ds(line, SUB), :], axis=1, mode="promise_in_bounds"
        )
        w_ref[i * SUB : (i + 1) * SUB, :] = weights
        feat = feat_ref[i * BLK : (i + 1) * BLK, :]
        turned = feat.T
        scaled = jnp.concatenate(
            [
                (turned[:, c * LANES : (c + 1) * LANES].astype(F32) * weights[c : c + 1, :]).astype(
                    jnp.bfloat16
                )
                for c in range(SUB)
            ],
            axis=1,
        )
        head = heads[line, 0]
        acc[head] += jnp.dot(scaled, feat, preferred_element_type=F32)
        here = tgt[pl.ds(line, SUB), :]
        spread = jnp.concatenate([jnp.where(row == c, here, 0.0) for c in range(SUB)], axis=1)
        vec[head] += lax.dot_general(
            spread.astype(jnp.bfloat16),
            scaled,
            (((1,), (1,)), ((), ())),
            preferred_element_type=F32,
        )

    @pl.when(step == pl.num_programs(0) - 1)
    def _():
        left = lax.broadcasted_iota(jnp.int32, (64, LANES), 1) < 64

        @pl.loop(0, HEADS, unroll=4)
        def _(h):
            g11, g22 = acc[h, 0:128, 0:128], acc[h, 128:256, 128:256]
            lower1, top1 = half_tiles(0.5 * (g11 + g11.T))
            lower2, top2 = half_tiles(0.5 * (g22 + g22.T))
            out_ref[h, 0:64, :] = jnp.where(left, top1, pltpu.roll(top2, 64, 1))
            out_ref[h, 64:128, :] = lower1
            out_ref[h, 128:192, :] = lower2
            out_ref[h, 192:320, :] = 0.5 * (acc[h, 128:256, 0:128] + acc[h, 0:128, 128:256].T)
            total = jnp.sum(vec[h], axis=0, keepdims=True)
            out_ref[h, VEC_ROW:PACK_ROWS, :] = jnp.zeros((PACK_ROWS - VEC_ROW, LANES), F32)
            out_ref[h, VEC_ROW : VEC_ROW + 1, :] = total[:, 0:128]
            out_ref[h, VEC_ROW + 1 : VEC_ROW + 2, :] = total[:, 128:256]


def reduce_kernel(plan, g_ref, out_ref, acc, first, fin, *rest):
    core_bits, orders, groups = plan
    stage_count = len(orders[0])
    count = len(CHAINS)
    bufs = [rest[c * stage_count : (c + 1) * stage_count] for c in range(count)]
    send, recv = rest[-2:]
    half = PACK_ROWS // 2
    core = bit_value(core_bits[0])
    own = [pl.ds(start, size) for start, size in CHAINS]
    mine = [pl.ds(pl.multiple_of(core * half + start, 8), size) for start, size in CHAINS]
    theirs = [pl.ds(pl.multiple_of((1 - core) * half + start, 8), size) for start, size in CHAINS]
    greet(groups)
    sent = []
    flying = [[] for _ in range(count)]
    index = [[slice(None)] * HEAD_BITS for _ in range(count)]

    def push(src, dst, chain, stage, bits, move):
        copy = pltpu.make_async_remote_copy(
            src_ref=src,
            dst_ref=dst,
            send_sem=send.at[chain, stage, move - 1],
            recv_sem=recv.at[chain, stage, move - 1],
            device_id=partner(bits, move),
            device_id_type=MESH,
        )
        copy.start()
        sent.append(copy)
        flying[chain].append(copy)

    def take(c, stage):
        arrived, flying[c] = flying[c], []
        place = (*index[c], own[c])
        for i, copy in enumerate(arrived):
            copy.wait_recv()
            if stage > 0 and not orders[c % 2][stage - 1][1]:
                copy.wait_send()
                sent[:] = [other for other in sent if other is not copy]
            if stage == 0:
                acc[place] = g_ref[:, :, :, :, mine[c], :] + first[place]
            else:
                acc[place] = acc[place] + bufs[c][stage - 1][i]

    def give(c, stage):
        if stage == stage_count:
            push(acc.at[(*index[c], own[c])], fin.at[own[c]], c, stage + 1, core_bits, 1)
            return
        bits, dims = orders[c % 2][stage]
        kept = list(index[c])
        for move in reversed(moves_of(bits)):
            away = list(index[c])
            for i, dim in enumerate(dims):
                away[dim] = flipped(bits[i], i, move)
                kept[dim] = bit_value(bits[i])
            push(acc.at[(*away, own[c])], bufs[c][stage].at[move - 1], c, stage + 1, bits, move)
        flying[c].reverse()
        index[c] = kept

    every = [slice(None)] * HEAD_BITS
    for c in range(count):
        push(g_ref.at[(*every, theirs[c])], first.at[(*every, own[c])], c, 0, core_bits, 1)
    for stage in range(stage_count + 1):
        for c in range(count):
            take(c, stage)
            give(c, stage)
    for c in range(count):
        for copy in flying[c]:
            copy.wait_recv()
        out_ref[mine[c], :] = acc[(*index[c], own[c])]
        out_ref[theirs[c], :] = fin[own[c], :]
    for copy in sent:
        copy.wait_send()


def gather_kernel(plan, x_ref, out_ref, send, recv, send_core, recv_core):
    core_bits, orders, groups = plan
    count = len(CHAINS)
    half = PACK_ROWS // 2
    core = bit_value(core_bits[0])
    mine = [pl.ds(pl.multiple_of(core * half + start, 8), size) for start, size in CHAINS]
    own = [None] * HEAD_BITS
    for bits, dims in orders[0]:
        for bit, dim in zip(bits, dims):
            own[dim] = bit_value(bit)
    out_ref[(*own,)] = x_ref[...]
    greet(groups)
    sent, late = [], []

    def push(place, chain, bits, move, send_sem, recv_sem):
        view = out_ref.at[(*place, mine[chain])]
        copy = pltpu.make_async_remote_copy(
            src_ref=view,
            dst_ref=view,
            send_sem=send_sem,
            recv_sem=recv_sem,
            device_id=partner(bits, move),
            device_id_type=MESH,
        )
        copy.start()
        sent.append(copy)
        return copy

    index = [list(own) for _ in range(count)]
    flying = [[] for _ in range(count)]
    stage_count = len(orders[0])

    def give(c, stage):
        if stage < stage_count:
            bits, dims = orders[c % 2][stage]
            flying[c] = [
                (
                    move,
                    push(
                        index[c],
                        c,
                        bits,
                        move,
                        send.at[c, stage, move - 1],
                        recv.at[c, stage, move - 1],
                    ),
                )
                for move in reversed(moves_of(bits))
            ]

    def take(c, stage):
        bits, dims = orders[c % 2][stage]
        fresh = []
        for move, copy in reversed(flying[c]):
            copy.wait_recv()
            news = list(index[c])
            for i, dim in enumerate(dims):
                news[dim] = flipped(bits[i], i, move)
            fresh.append((move, news))
        for dim in dims:
            index[c][dim] = slice(None)
        give(c, stage + 1)
        for move, news in fresh:
            late.append(
                push(
                    news,
                    c,
                    core_bits,
                    1,
                    send_core.at[c, stage, move - 1],
                    recv_core.at[c, stage, move - 1],
                )
            )

    turn = (2, 3, 0, 1)
    for c in turn:
        give(c, 0)
    for stage in range(stage_count):
        for c in turn:
            take(c, stage)
    for copy in late:
        copy.wait_recv()
    for copy in sent:
        copy.wait_send()


def mm(a, b, dims):
    return lax.dot_general(a, b, (dims, ((), ())), precision=HIGHEST, preferred_element_type=F32)


def eliminate(matrix, offset):
    groups = matrix.shape[0] // 8
    rows = [matrix[8 * g : 8 * g + 8, :] for g in range(groups)]
    below = lax.broadcasted_iota(jnp.int32, (8, LANES), 0)
    for p in range(groups):
        columns = [offset + 8 * p + k for k in range(8)]
        pivots = [None] * 8
        across = [[None] * 8 for _ in range(8)]
        lines = [None] * 8
        for g in range(p, groups):
            cols = [jnp.broadcast_to(rows[g][:, j : j + 1], (8, LANES)) for j in columns]
            for k in range(8):
                if g == p:
                    pivots[k] = 1.0 / cols[k][k : k + 1, :]
                    lines[k] = rows[p][k : k + 1, :]
                    for m in range(k + 1, 8):
                        across[k][m] = cols[m][k : k + 1, :]
                factor = cols[k] * pivots[k]
                if g == p:
                    factor = jnp.where(below > k, factor, 0.0)
                for m in range(k + 1, 8):
                    cols[m] = cols[m] - factor * across[k][m]
                rows[g] = rows[g] - factor * lines[k]
    done = jnp.concatenate(rows, axis=0)
    lane = lax.broadcasted_iota(jnp.int32, done.shape, 1)
    row = lax.broadcasted_iota(jnp.int32, done.shape, 0)
    diagonal = jnp.sum(jnp.where(lane == row + offset, done, 0.0), axis=1, keepdims=True)
    return done * (1.0 / jnp.sqrt(diagonal))


def inverse_factor_128(top, bottom):
    lane = lax.broadcasted_iota(jnp.int32, (64, LANES), 1)
    row = lax.broadcasted_iota(jnp.int32, (64, LANES), 0)
    low = lane < 64
    eye = (lane == row + 64).astype(F32)
    none = jnp.zeros((64, LANES), F32)
    first = eliminate(jnp.where(low, top, eye), 0)
    x1 = jnp.where(low, pltpu.roll(first, 64, 1), 0.0)
    x1_full = jnp.concatenate([x1, none], axis=0)
    lower = mm(bottom, x1_full, ((1,), (1,)))
    square = mm(lower, jnp.concatenate([lower, none], axis=0), ((1,), (1,)))
    second = eliminate(jnp.where(low, pltpu.roll(bottom, 64, 1) - square, eye), 0)
    x2 = jnp.where(low, 0.0, second)
    across = mm(lower, x1_full, ((1,), (0,)))
    x21 = -mm(x2, jnp.concatenate([none, across], axis=0), ((1,), (0,)))
    return x1, x21 + x2


def factor_kernel(g_ref, out_ref):
    lane = lax.broadcasted_iota(jnp.int32, (64, LANES), 1)
    row = lax.broadcasted_iota(jnp.int32, (64, LANES), 0)
    low = lane < 64
    eye_top = (lane == row).astype(F32)
    eye_bottom = (lane == row + 64).astype(F32)
    tops = g_ref[0:64, :]
    top1, bottom1 = inverse_factor_128(tops + eye_top, g_ref[64:128, :] + eye_bottom)
    x1 = jnp.concatenate([top1, bottom1], axis=0)
    lower = mm(g_ref[192:320, :], x1, ((1,), (1,)))
    square = mm(lower, lower, ((1,), (1,)))
    top2, bottom2 = inverse_factor_128(
        pltpu.roll(tops, 64, 1) + eye_top - square[0:64, :],
        g_ref[128:192, :] + eye_bottom - square[64:128, :],
    )
    x2 = jnp.concatenate([top2, bottom2], axis=0)
    x21 = -mm(x2, mm(lower, x1, ((1,), (0,))), ((1,), (0,)))
    out_ref[0:64, :] = jnp.where(low, top1, pltpu.roll(top2, 64, 1))
    out_ref[64:128, :] = bottom1
    out_ref[128:192, :] = bottom2
    out_ref[192:320, :] = x21
    m1 = jnp.broadcast_to(g_ref[VEC_ROW : VEC_ROW + 1, :], (8, LANES))
    m2 = jnp.broadcast_to(g_ref[VEC_ROW + 1 : VEC_ROW + 2, :], (8, LANES))
    in1 = mm(m1, x1, ((1,), (1,)))
    in2 = mm(m1, x21, ((1,), (1,))) + mm(m2, x2, ((1,), (1,)))
    co1 = mm(in1, x1, ((1,), (0,))) + mm(in2, x21, ((1,), (0,)))
    co2 = mm(in2, x2, ((1,), (0,)))
    s1 = jnp.sum(x1 * x1, axis=0, keepdims=True) + jnp.sum(x21 * x21, axis=0, keepdims=True)
    s2 = jnp.sum(x2 * x2, axis=0, keepdims=True)
    out_ref[VEC_ROW:PACK_ROWS, :] = jnp.zeros((PACK_ROWS - VEC_ROW, LANES), F32)
    out_ref[VEC_ROW : VEC_ROW + 1, :] = co1[0:1, :] / jnp.sqrt(s1)
    out_ref[VEC_ROW + 1 : VEC_ROW + 2, :] = co2[0:1, :] / jnp.sqrt(s2)


def leverage_kernel(scale, place_ref, heads_ref, feat_ref, w_ref, inv_ref, lev_ref, z_ref, piece_ref):
    step = pl.program_id(0)
    per = feat_ref.shape[0] // BLK

    @pl.when(step == 0)
    def _():
        z_ref[:, 0:128] = inv_ref[:, VEC_ROW, :]
        z_ref[:, 128:256] = inv_ref[:, VEC_ROW + 1, :]
        count = piece_ref.shape[1]
        start = place_ref[0] * count
        root = math.sqrt(scale * 2 * LANES)
        low = lax.broadcasted_iota(jnp.int32, (count, LANES), 1) < 64

        def rows(first):
            return inv_ref[:, pl.ds(pl.multiple_of(first, 8), count), :] * root

        @pl.when(start < 64)
        def _():
            piece_ref[:, :, 0:128] = jnp.where(low, rows(start), 0.0)

        @pl.when(jnp.logical_and(start >= 64, start < 128))
        def _():
            piece_ref[:, :, 0:128] = rows(start)

        @pl.when(start < 128)
        def _():
            piece_ref[:, :, 128:256] = jnp.zeros((HEADS, count, LANES), F32)

        @pl.when(start >= 128)
        def _():
            piece_ref[:, :, 0:128] = rows(start + 64)

        @pl.when(jnp.logical_and(start >= 128, start < 192))
        def _():
            for h in range(HEADS):
                part = inv_ref[h, pl.ds(pl.multiple_of(start - 128, 8), count), :] * root
                piece_ref[h, :, 128:256] = jnp.where(low, pltpu.roll(part, 64, 1), 0.0)

        @pl.when(start >= 192)
        def _():
            piece_ref[:, :, 128:256] = rows(start - 64)

    low = lax.broadcasted_iota(jnp.int32, (64, LANES), 1) < 64
    zero = jnp.zeros((128, 128), jnp.bfloat16)
    for i in range(per):
        head = heads_ref[i * SUB, 0]
        tops = inv_ref[head, 0:64, :]
        x1 = jnp.concatenate([jnp.where(low, tops, 0.0), inv_ref[head, 64:128, :]], axis=0)
        x2 = jnp.concatenate(
            [jnp.where(low, pltpu.roll(tops, 64, 1), 0.0), inv_ref[head, 128:192, :]], axis=0
        )
        x21 = inv_ref[head, 192:320, :]
        x1, x21, x2 = (x.astype(jnp.bfloat16) for x in (x1, x21, x2))
        inverse = jnp.concatenate(
            [jnp.concatenate([x1, zero], axis=1), jnp.concatenate([x21, x2], axis=1)], axis=0
        )
        projected = lax.dot_general(
            feat_ref[i * BLK : (i + 1) * BLK, :],
            inverse,
            (((1,), (1,)), ((), ())),
            preferred_element_type=F32,
        )
        one, two = projected[:, 0:128], projected[:, 128:256]
        squares = one * one + two * two
        for c in range(SUB):
            line = jnp.sum(squares[c * LANES : (c + 1) * LANES, :].T, axis=0, keepdims=True)
            here = i * SUB + c
            lev_ref[here : here + 1, :] = w_ref[here : here + 1, :] * line * scale


def local(mesh_shape, features, targets, station_ids, lead_heads, station_weight):
    row_count, width = features.shape
    blocks = row_count // BLK
    lines = row_count // LANES
    tm = mesh_shape["tm"]
    total_rows = row_count * mesh_shape["station"] * tm
    scale = total_rows / (HEADS * width)
    ids = station_ids.reshape(lines, LANES)
    heads = lead_heads.reshape(lines, LANES)
    goals = targets.reshape(lines, LANES)
    per = math.gcd(blocks, 4)
    head_spec = pl.BlockSpec((per * SUB, LANES), lambda b: (b, 0), memory_space=pltpu.SMEM)
    line_spec = pl.BlockSpec((per * SUB, LANES), lambda b: (b, 0))
    feat_spec = pl.BlockSpec((per * BLK, width), lambda b: (b, 0))
    away = pl.BlockSpec(memory_space=pltpu.HBM)
    big = 48 * 1024 * 1024
    packed, weights = pl.pallas_call(
        gram_kernel,
        grid=(blocks // per,),
        in_specs=[
            away,
            feat_spec,
            away,
            away,
            away,
        ],
        out_specs=[pl.BlockSpec((HEADS, PACK_ROWS, LANES), lambda b: (0, 0, 0)), line_spec],
        out_shape=[
            jax.ShapeDtypeStruct((HEADS, PACK_ROWS, LANES), F32),
            jax.ShapeDtypeStruct((lines, LANES), F32),
        ],
        scratch_shapes=[
            pltpu.VMEM((HEADS, width, width), F32),
            pltpu.VMEM((HEADS, 8, width), F32),
            pltpu.SMEM((lines, LANES), jnp.int32),
            pltpu.VMEM((lines, LANES), jnp.int32),
            pltpu.VMEM((lines, LANES), jnp.bfloat16),
            pltpu.VMEM((lines, LANES), F32),
            pltpu.VMEM(station_weight.shape, F32),
            pltpu.SemaphoreType.DMA((4,)),
        ],
        compiler_params=pltpu.CompilerParams(vmem_limit_bytes=big),
        name="gram",
    )(heads, features, ids, goals, station_weight)

    core_bit, owner, rest = bits_of(mesh_shape)
    core = (core_bit,)
    x, y = ((owner[0],), (0,)), ((owner[1],), (1,))
    z = ((owner[2], owner[3]), (2, 3))
    tail = [((bit,), ()) for bit in rest]
    down = ([x, y, z] + tail, [y, x, z] + tail)
    up = ([z, y, x], [z, x, y])
    groups_up = [core] + [bits for bits, _ in up[0]]
    groups_down = groups_up + [bits for bits, _ in tail]
    partners = 3
    dims = (2,) * HEAD_BITS
    half = PACK_ROWS // 2
    count = len(CHAINS)
    buffers = []
    for c, (_, size) in enumerate(CHAINS):
        free = HEAD_BITS
        for bits, spots in down[c % 2]:
            free -= len(spots)
            shape = (len(moves_of(bits)),) + (2,) * free + (size, LANES)
            buffers.append(pltpu.VMEM(shape, F32))
    vmem = pl.BlockSpec(memory_space=pltpu.VMEM)
    summed = pl.pallas_call(
        functools.partial(reduce_kernel, (core, down, groups_down)),
        out_shape=jax.ShapeDtypeStruct((PACK_ROWS, LANES), F32),
        in_specs=[vmem],
        out_specs=vmem,
        scratch_shapes=[
            pltpu.VMEM((*dims, half, LANES), F32),
            pltpu.VMEM((*dims, half, LANES), F32),
            pltpu.VMEM((half, LANES), F32),
            *buffers,
            pltpu.SemaphoreType.DMA((count, len(down[0]) + 2, partners)),
            pltpu.SemaphoreType.DMA((count, len(down[0]) + 2, partners)),
        ],
        compiler_params=pltpu.CompilerParams(
            collective_id=0, has_side_effects=True, vmem_limit_bytes=big
        ),
        name="reduce",
    )(packed.reshape(*dims, PACK_ROWS, LANES))

    solved = pl.pallas_call(
        factor_kernel,
        out_shape=jax.ShapeDtypeStruct((PACK_ROWS, LANES), F32),
        in_specs=[vmem],
        out_specs=vmem,
        compiler_params=pltpu.CompilerParams(vmem_limit_bytes=big),
        name="factor",
    )(summed)

    everyone = pl.pallas_call(
        functools.partial(gather_kernel, (core, up, groups_up)),
        out_shape=jax.ShapeDtypeStruct((*dims, PACK_ROWS, LANES), F32),
        in_specs=[vmem],
        out_specs=vmem,
        scratch_shapes=[
            pltpu.SemaphoreType.DMA((count, len(up[0]), partners)),
            pltpu.SemaphoreType.DMA((count, len(up[0]), partners)),
            pltpu.SemaphoreType.DMA((count, len(up[0]), partners)),
            pltpu.SemaphoreType.DMA((count, len(up[0]), partners)),
        ],
        compiler_params=pltpu.CompilerParams(
            collective_id=1, has_side_effects=True, vmem_limit_bytes=big
        ),
        name="gather",
    )(solved).reshape(HEADS, PACK_ROWS, LANES)

    piece_rows = width // tm
    place = lax.axis_index("tm").reshape(1).astype(jnp.int32)
    leverage, zscores, pieces = pl.pallas_call(
        functools.partial(leverage_kernel, scale),
        grid=(blocks // per,),
        in_specs=[
            pl.BlockSpec(memory_space=pltpu.SMEM),
            head_spec,
            feat_spec,
            line_spec,
            pl.BlockSpec((HEADS, PACK_ROWS, LANES), lambda b: (0, 0, 0)),
        ],
        out_specs=[
            line_spec,
            pl.BlockSpec((HEADS, width), lambda b: (0, 0)),
            pl.BlockSpec((HEADS, piece_rows, width), lambda b: (0, 0, 0)),
        ],
        out_shape=[
            jax.ShapeDtypeStruct((lines, LANES), F32),
            jax.ShapeDtypeStruct((HEADS, width), F32),
            jax.ShapeDtypeStruct((HEADS, piece_rows, width), F32),
        ],
        compiler_params=pltpu.CompilerParams(vmem_limit_bytes=big),
        name="leverage",
    )(place, heads, features, weights, everyone)
    return (leverage.reshape(row_count), zscores, pieces)


def solution(mesh):
    return jax.shard_map(
        functools.partial(local, dict(mesh.shape)),
        mesh=mesh,
        in_specs=(
            P(("station", "tm"), None),
            P(("station", "tm")),
            P(("station", "tm")),
            P(("station", "tm")),
            P("station", None),
        ),
        out_specs=(P(("station", "tm")), P(), P(None, "tm", None)),
        check_vma=False,
    )
```

```python
import functools
import math

import jax
import jax.numpy as jnp
from jax import lax
from jax.experimental import pallas as pl
from jax.experimental.pallas import tpu as pltpu
from jax.sharding import PartitionSpec as P

HEADS = 16
BLK = 1024
LANES = 128
SUB = BLK // LANES
HEAD_BITS = 4
F32 = jnp.float32
HIGHEST = lax.Precision.HIGHEST
MESH = pl.DeviceIdType.MESH
PACK_ROWS = 336
VEC_ROW = 320
CHAINS = ((0, 32), (32, 32), (64, 56), (120, 48))


def bits_of(mesh_shape):
    station, tm = mesh_shape["station"], mesh_shape["tm"]
    core = ("tm", 1)
    owner = [("station", 1), ("tm", 2), ("tm", 4), ("tm", 8)]
    rest = [("station", s) for s in (2**i for i in range(1, 16)) if s < station]
    rest += [("tm", s) for s in (2**i for i in range(4, 16)) if s < tm]
    return core, owner, rest


def bit_value(bit):
    return lax.rem(lax.div(lax.axis_index(bit[0]), bit[1]), 2)


def moves_of(bits):
    return range(1, 2 ** len(bits))


def partner(bits, move):
    place = {}
    for i, (axis, step) in enumerate(bits):
        if (move >> i) & 1:
            here = place.get(axis, lax.axis_index(axis))
            place[axis] = here + (1 - 2 * bit_value((axis, step))) * step
    return place


def flipped(bit, i, move):
    value = bit_value(bit)
    return 1 - value if (move >> i) & 1 else value


def greet(groups):
    barrier = pltpu.get_barrier_semaphore()
    met = 0
    for bits in groups:
        for move in moves_of(bits):
            pl.semaphore_signal(
                barrier, inc=1, device_id=partner(bits, move), device_id_type=MESH
            )
            met += 1
    pl.semaphore_wait(barrier, met)


def half_tiles(full):
    return full[64:128, :], full[0:64, :]


def gram_kernel(
    feat_ref, code_ref, tgt_ref, table_ref, out_ref, w_ref, acc, vec, codes, sem
):
    step = pl.program_id(0)
    per = feat_ref.shape[0] // BLK

    @pl.when(step == 0)
    def _():
        copy = pltpu.make_async_copy(code_ref, codes, sem)
        copy.start()
        acc[...] = jnp.zeros_like(acc)
        vec[...] = jnp.zeros_like(vec)
        copy.wait()

    lookup = jnp.broadcast_to(table_ref[...], (SUB, LANES))
    row = lax.broadcasted_iota(jnp.int32, (SUB, LANES), 0)
    for i in range(per):
        line = pl.multiple_of((step * per + i) * SUB, SUB)
        ids = jnp.bitwise_and(code_ref[pl.ds(line, SUB), :], LANES - 1)
        weights = jnp.take_along_axis(lookup, ids, axis=1, mode="promise_in_bounds")
        w_ref[i * SUB : (i + 1) * SUB, :] = weights
        feat = feat_ref[i * BLK : (i + 1) * BLK, :]
        turned = feat.T
        scaled = jnp.concatenate(
            [
                (turned[:, c * LANES : (c + 1) * LANES].astype(F32) * weights[c : c + 1, :]).astype(
                    jnp.bfloat16
                )
                for c in range(SUB)
            ],
            axis=1,
        )
        head = lax.div(codes[line, 0], LANES)
        acc[head] += jnp.dot(scaled, feat, preferred_element_type=F32)
        here = tgt_ref[pl.ds(line, SUB), :]
        spread = jnp.concatenate([jnp.where(row == c, here, 0.0) for c in range(SUB)], axis=1)
        vec[head] += lax.dot_general(
            spread.astype(jnp.bfloat16),
            scaled,
            (((1,), (1,)), ((), ())),
            preferred_element_type=F32,
        )

    @pl.when(step == pl.num_programs(0) - 1)
    def _():
        left = lax.broadcasted_iota(jnp.int32, (64, LANES), 1) < 64

        @pl.loop(0, HEADS, unroll=4)
        def _(h):
            g11, g22 = acc[h, 0:128, 0:128], acc[h, 128:256, 128:256]
            lower1, top1 = half_tiles(0.5 * (g11 + g11.T))
            lower2, top2 = half_tiles(0.5 * (g22 + g22.T))
            out_ref[h, 0:64, :] = jnp.where(left, top1, pltpu.roll(top2, 64, 1))
            out_ref[h, 64:128, :] = lower1
            out_ref[h, 128:192, :] = lower2
            out_ref[h, 192:320, :] = 0.5 * (acc[h, 128:256, 0:128] + acc[h, 0:128, 128:256].T)
            total = jnp.sum(vec[h], axis=0, keepdims=True)
            out_ref[h, VEC_ROW:PACK_ROWS, :] = jnp.zeros((PACK_ROWS - VEC_ROW, LANES), F32)
            out_ref[h, VEC_ROW : VEC_ROW + 1, :] = total[:, 0:128]
            out_ref[h, VEC_ROW + 1 : VEC_ROW + 2, :] = total[:, 128:256]


def reduce_kernel(plan, g_ref, out_ref, acc, first, fin, *rest):
    core_bits, orders, groups = plan
    stage_count = len(orders[0])
    count = len(CHAINS)
    bufs = [rest[c * stage_count : (c + 1) * stage_count] for c in range(count)]
    send, recv = rest[-2:]
    half = PACK_ROWS // 2
    core = bit_value(core_bits[0])
    own = [pl.ds(start, size) for start, size in CHAINS]
    mine = [pl.ds(pl.multiple_of(core * half + start, 8), size) for start, size in CHAINS]
    theirs = [pl.ds(pl.multiple_of((1 - core) * half + start, 8), size) for start, size in CHAINS]
    greet(groups)
    sent = []
    flying = [[] for _ in range(count)]
    index = [[slice(None)] * HEAD_BITS for _ in range(count)]

    def push(src, dst, chain, stage, bits, move):
        copy = pltpu.make_async_remote_copy(
            src_ref=src,
            dst_ref=dst,
            send_sem=send.at[chain, stage, move - 1],
            recv_sem=recv.at[chain, stage, move - 1],
            device_id=partner(bits, move),
            device_id_type=MESH,
        )
        copy.start()
        sent.append(copy)
        flying[chain].append(copy)

    def take(c, stage):
        arrived, flying[c] = flying[c], []
        place = (*index[c], own[c])
        for i, copy in enumerate(arrived):
            copy.wait_recv()
            if stage > 0 and not orders[c % 2][stage - 1][1]:
                copy.wait_send()
                sent[:] = [other for other in sent if other is not copy]
            if stage == 0:
                acc[place] = g_ref[:, :, :, :, mine[c], :] + first[place]
            else:
                acc[place] = acc[place] + bufs[c][stage - 1][i]

    def give(c, stage):
        if stage == stage_count:
            push(acc.at[(*index[c], own[c])], fin.at[own[c]], c, stage + 1, core_bits, 1)
            return
        bits, dims = orders[c % 2][stage]
        kept = list(index[c])
        for move in reversed(moves_of(bits)):
            away = list(index[c])
            for i, dim in enumerate(dims):
                away[dim] = flipped(bits[i], i, move)
                kept[dim] = bit_value(bits[i])
            push(acc.at[(*away, own[c])], bufs[c][stage].at[move - 1], c, stage + 1, bits, move)
        flying[c].reverse()
        index[c] = kept

    every = [slice(None)] * HEAD_BITS
    for c in range(count):
        push(g_ref.at[(*every, theirs[c])], first.at[(*every, own[c])], c, 0, core_bits, 1)
    for stage in range(stage_count + 1):
        for c in range(count):
            take(c, stage)
            give(c, stage)
    for c in range(count):
        for copy in flying[c]:
            copy.wait_recv()
        out_ref[mine[c], :] = acc[(*index[c], own[c])]
        out_ref[theirs[c], :] = fin[own[c], :]
    for copy in sent:
        copy.wait_send()


def gather_kernel(plan, x_ref, out_ref, send, recv, send_core, recv_core):
    core_bits, orders, groups = plan
    count = len(CHAINS)
    half = PACK_ROWS // 2
    core = bit_value(core_bits[0])
    mine = [pl.ds(pl.multiple_of(core * half + start, 8), size) for start, size in CHAINS]
    own = [None] * HEAD_BITS
    for bits, dims in orders[0]:
        for bit, dim in zip(bits, dims):
            own[dim] = bit_value(bit)
    out_ref[(*own,)] = x_ref[...]
    greet(groups)
    sent, late = [], []

    def push(place, chain, bits, move, send_sem, recv_sem):
        view = out_ref.at[(*place, mine[chain])]
        copy = pltpu.make_async_remote_copy(
            src_ref=view,
            dst_ref=view,
            send_sem=send_sem,
            recv_sem=recv_sem,
            device_id=partner(bits, move),
            device_id_type=MESH,
        )
        copy.start()
        sent.append(copy)
        return copy

    index = [list(own) for _ in range(count)]
    flying = [[] for _ in range(count)]
    stage_count = len(orders[0])

    def give(c, stage):
        if stage < stage_count:
            bits, dims = orders[c % 2][stage]
            flying[c] = [
                (
                    move,
                    push(
                        index[c],
                        c,
                        bits,
                        move,
                        send.at[c, stage, move - 1],
                        recv.at[c, stage, move - 1],
                    ),
                )
                for move in reversed(moves_of(bits))
            ]

    def take(c, stage):
        bits, dims = orders[c % 2][stage]
        fresh = []
        for move, copy in reversed(flying[c]):
            copy.wait_recv()
            news = list(index[c])
            for i, dim in enumerate(dims):
                news[dim] = flipped(bits[i], i, move)
            fresh.append((move, news))
        for dim in dims:
            index[c][dim] = slice(None)
        give(c, stage + 1)
        for move, news in fresh:
            late.append(
                push(
                    news,
                    c,
                    core_bits,
                    1,
                    send_core.at[c, stage, move - 1],
                    recv_core.at[c, stage, move - 1],
                )
            )

    turn = (2, 3, 0, 1)
    for c in turn:
        give(c, 0)
    for stage in range(stage_count):
        for c in turn:
            take(c, stage)
    for copy in late:
        copy.wait_recv()
    for copy in sent:
        copy.wait_send()


def mm(a, b, dims):
    return lax.dot_general(a, b, (dims, ((), ())), precision=HIGHEST, preferred_element_type=F32)


def eliminate(matrix, offset):
    groups = matrix.shape[0] // 8
    rows = [matrix[8 * g : 8 * g + 8, :] for g in range(groups)]
    below = lax.broadcasted_iota(jnp.int32, (8, LANES), 0)
    for p in range(groups):
        columns = [offset + 8 * p + k for k in range(8)]
        pivots = [None] * 8
        across = [[None] * 8 for _ in range(8)]
        lines = [None] * 8
        for g in range(p, groups):
            cols = [jnp.broadcast_to(rows[g][:, j : j + 1], (8, LANES)) for j in columns]
            for k in range(8):
                if g == p:
                    if k % 2 == 0:
                        a = cols[k][k : k + 1, :]
                        b = cols[k + 1][k : k + 1, :]
                        d = cols[k + 1][k + 1 : k + 2, :]
                        pivots[k] = 1.0 / a
                        pivots[k + 1] = a * (1.0 / (a * d - b * b))
                    lines[k] = rows[p][k : k + 1, :]
                    for m in range(k + 1, 8):
                        across[k][m] = cols[m][k : k + 1, :]
                factor = cols[k] * pivots[k]
                if g == p:
                    factor = jnp.where(below > k, factor, 0.0)
                for m in range(k + 1, 8):
                    cols[m] = cols[m] - factor * across[k][m]
                rows[g] = rows[g] - factor * lines[k]
    done = jnp.concatenate(rows, axis=0)
    lane = lax.broadcasted_iota(jnp.int32, done.shape, 1)
    row = lax.broadcasted_iota(jnp.int32, done.shape, 0)
    diagonal = jnp.sum(jnp.where(lane == row + offset, done, 0.0), axis=1, keepdims=True)
    return done * (1.0 / jnp.sqrt(diagonal))


def inverse_factor_128(top, bottom):
    lane = lax.broadcasted_iota(jnp.int32, (64, LANES), 1)
    row = lax.broadcasted_iota(jnp.int32, (64, LANES), 0)
    low = lane < 64
    eye = (lane == row + 64).astype(F32)
    none = jnp.zeros((64, LANES), F32)
    first = eliminate(jnp.where(low, top, eye), 0)
    x1 = jnp.where(low, pltpu.roll(first, 64, 1), 0.0)
    x1_full = jnp.concatenate([x1, none], axis=0)
    lower = mm(bottom, x1_full, ((1,), (1,)))
    square = mm(lower, jnp.concatenate([lower, none], axis=0), ((1,), (1,)))
    second = eliminate(jnp.where(low, pltpu.roll(bottom, 64, 1) - square, eye), 0)
    x2 = jnp.where(low, 0.0, second)
    across = mm(lower, x1_full, ((1,), (0,)))
    x21 = -mm(x2, jnp.concatenate([none, across], axis=0), ((1,), (0,)))
    return x1, x21 + x2


def factor_kernel(g_ref, out_ref):
    lane = lax.broadcasted_iota(jnp.int32, (64, LANES), 1)
    row = lax.broadcasted_iota(jnp.int32, (64, LANES), 0)
    low = lane < 64
    eye_top = (lane == row).astype(F32)
    eye_bottom = (lane == row + 64).astype(F32)
    tops = g_ref[0:64, :]
    top1, bottom1 = inverse_factor_128(tops + eye_top, g_ref[64:128, :] + eye_bottom)
    x1 = jnp.concatenate([top1, bottom1], axis=0)
    lower = mm(g_ref[192:320, :], x1, ((1,), (1,)))
    square = mm(lower, lower, ((1,), (1,)))
    top2, bottom2 = inverse_factor_128(
        pltpu.roll(tops, 64, 1) + eye_top - square[0:64, :],
        g_ref[128:192, :] + eye_bottom - square[64:128, :],
    )
    x2 = jnp.concatenate([top2, bottom2], axis=0)
    x21 = -mm(x2, mm(lower, x1, ((1,), (0,))), ((1,), (0,)))
    out_ref[0:64, :] = jnp.where(low, top1, pltpu.roll(top2, 64, 1))
    out_ref[64:128, :] = bottom1
    out_ref[128:192, :] = bottom2
    out_ref[192:320, :] = x21
    m1 = jnp.broadcast_to(g_ref[VEC_ROW : VEC_ROW + 1, :], (8, LANES))
    m2 = jnp.broadcast_to(g_ref[VEC_ROW + 1 : VEC_ROW + 2, :], (8, LANES))
    in1 = mm(m1, x1, ((1,), (1,)))
    in2 = mm(m1, x21, ((1,), (1,))) + mm(m2, x2, ((1,), (1,)))
    co1 = mm(in1, x1, ((1,), (0,))) + mm(in2, x21, ((1,), (0,)))
    co2 = mm(in2, x2, ((1,), (0,)))
    s1 = jnp.sum(x1 * x1, axis=0, keepdims=True) + jnp.sum(x21 * x21, axis=0, keepdims=True)
    s2 = jnp.sum(x2 * x2, axis=0, keepdims=True)
    out_ref[VEC_ROW:PACK_ROWS, :] = jnp.zeros((PACK_ROWS - VEC_ROW, LANES), F32)
    out_ref[VEC_ROW : VEC_ROW + 1, :] = co1[0:1, :] / jnp.sqrt(s1)
    out_ref[VEC_ROW + 1 : VEC_ROW + 2, :] = co2[0:1, :] / jnp.sqrt(s2)


def leverage_kernel(scale, place_ref, heads_ref, feat_ref, w_ref, inv_ref, lev_ref, z_ref, piece_ref):
    step = pl.program_id(0)
    per = feat_ref.shape[0] // BLK

    @pl.when(step == 0)
    def _():
        z_ref[:, 0:128] = inv_ref[:, VEC_ROW, :]
        z_ref[:, 128:256] = inv_ref[:, VEC_ROW + 1, :]
        count = piece_ref.shape[1]
        start = place_ref[0] * count
        root = math.sqrt(scale * 2 * LANES)
        low = lax.broadcasted_iota(jnp.int32, (count, LANES), 1) < 64

        def rows(first):
            return inv_ref[:, pl.ds(pl.multiple_of(first, 8), count), :] * root

        @pl.when(start < 64)
        def _():
            piece_ref[:, :, 0:128] = jnp.where(low, rows(start), 0.0)

        @pl.when(jnp.logical_and(start >= 64, start < 128))
        def _():
            piece_ref[:, :, 0:128] = rows(start)

        @pl.when(start < 128)
        def _():
            piece_ref[:, :, 128:256] = jnp.zeros((HEADS, count, LANES), F32)

        @pl.when(start >= 128)
        def _():
            piece_ref[:, :, 0:128] = rows(start + 64)

        @pl.when(jnp.logical_and(start >= 128, start < 192))
        def _():
            for h in range(HEADS):
                part = inv_ref[h, pl.ds(pl.multiple_of(start - 128, 8), count), :] * root
                piece_ref[h, :, 128:256] = jnp.where(low, pltpu.roll(part, 64, 1), 0.0)

        @pl.when(start >= 192)
        def _():
            piece_ref[:, :, 128:256] = rows(start - 64)

    low = lax.broadcasted_iota(jnp.int32, (64, LANES), 1) < 64
    zero = jnp.zeros((128, 128), jnp.bfloat16)
    for i in range(per):
        head = heads_ref[i * SUB, 0]
        tops = inv_ref[head, 0:64, :]
        x1 = jnp.concatenate([jnp.where(low, tops, 0.0), inv_ref[head, 64:128, :]], axis=0)
        x2 = jnp.concatenate(
            [jnp.where(low, pltpu.roll(tops, 64, 1), 0.0), inv_ref[head, 128:192, :]], axis=0
        )
        x21 = inv_ref[head, 192:320, :]
        x1, x21, x2 = (x.astype(jnp.bfloat16) for x in (x1, x21, x2))
        inverse = jnp.concatenate(
            [jnp.concatenate([x1, zero], axis=1), jnp.concatenate([x21, x2], axis=1)], axis=0
        )
        projected = lax.dot_general(
            feat_ref[i * BLK : (i + 1) * BLK, :],
            inverse,
            (((1,), (1,)), ((), ())),
            preferred_element_type=F32,
        )
        one, two = projected[:, 0:128], projected[:, 128:256]
        squares = one * one + two * two
        for c in range(SUB):
            line = jnp.sum(squares[c * LANES : (c + 1) * LANES, :].T, axis=0, keepdims=True)
            here = i * SUB + c
            lev_ref[here : here + 1, :] = w_ref[here : here + 1, :] * line * scale


def local(mesh_shape, features, targets, station_ids, lead_heads, station_weight):
    row_count, width = features.shape
    blocks = row_count // BLK
    lines = row_count // LANES
    tm = mesh_shape["tm"]
    total_rows = row_count * mesh_shape["station"] * tm
    scale = total_rows / (HEADS * width)
    heads = lead_heads.reshape(lines, LANES)
    codes = (lead_heads * LANES + station_ids).reshape(lines, LANES)
    goals = targets.astype(F32).reshape(lines, LANES)
    per = math.gcd(blocks, 4)
    head_spec = pl.BlockSpec((per * SUB, LANES), lambda b: (b, 0), memory_space=pltpu.SMEM)
    line_spec = pl.BlockSpec((per * SUB, LANES), lambda b: (b, 0))
    feat_spec = pl.BlockSpec((per * BLK, width), lambda b: (b, 0))
    big = 48 * 1024 * 1024
    packed, weights = pl.pallas_call(
        gram_kernel,
        grid=(blocks // per,),
        in_specs=[
            feat_spec,
            pl.BlockSpec((lines, LANES), lambda b: (0, 0)),
            pl.BlockSpec((lines, LANES), lambda b: (0, 0)),
            pl.BlockSpec((1, LANES), lambda b: (0, 0)),
        ],
        out_specs=[pl.BlockSpec((HEADS, PACK_ROWS, LANES), lambda b: (0, 0, 0)), line_spec],
        out_shape=[
            jax.ShapeDtypeStruct((HEADS, PACK_ROWS, LANES), F32),
            jax.ShapeDtypeStruct((lines, LANES), F32),
        ],
        scratch_shapes=[
            pltpu.VMEM((HEADS, width, width), F32),
            pltpu.VMEM((HEADS, 8, width), F32),
            pltpu.SMEM((lines, LANES), jnp.int32),
            pltpu.SemaphoreType.DMA,
        ],
        compiler_params=pltpu.CompilerParams(vmem_limit_bytes=big),
        name="gram",
    )(features, codes, goals, station_weight)

    core_bit, owner, rest = bits_of(mesh_shape)
    core = (core_bit,)
    x, y = ((owner[0],), (0,)), ((owner[1],), (1,))
    z = ((owner[2], owner[3]), (2, 3))
    tail = [((bit,), ()) for bit in rest]
    down = ([x, y, z] + tail, [y, x, z] + tail)
    up = ([z, y, x], [z, x, y])
    groups_up = [core] + [bits for bits, _ in up[0]]
    groups_down = groups_up + [bits for bits, _ in tail]
    partners = 3
    dims = (2,) * HEAD_BITS
    half = PACK_ROWS // 2
    count = len(CHAINS)
    buffers = []
    for c, (_, size) in enumerate(CHAINS):
        free = HEAD_BITS
        for bits, spots in down[c % 2]:
            free -= len(spots)
            shape = (len(moves_of(bits)),) + (2,) * free + (size, LANES)
            buffers.append(pltpu.VMEM(shape, F32))
    vmem = pl.BlockSpec(memory_space=pltpu.VMEM)
    summed = pl.pallas_call(
        functools.partial(reduce_kernel, (core, down, groups_down)),
        out_shape=jax.ShapeDtypeStruct((PACK_ROWS, LANES), F32),
        in_specs=[vmem],
        out_specs=vmem,
        scratch_shapes=[
            pltpu.VMEM((*dims, half, LANES), F32),
            pltpu.VMEM((*dims, half, LANES), F32),
            pltpu.VMEM((half, LANES), F32),
            *buffers,
            pltpu.SemaphoreType.DMA((count, len(down[0]) + 2, partners)),
            pltpu.SemaphoreType.DMA((count, len(down[0]) + 2, partners)),
        ],
        compiler_params=pltpu.CompilerParams(
            collective_id=0, has_side_effects=True, vmem_limit_bytes=big
        ),
        name="reduce",
    )(packed.reshape(*dims, PACK_ROWS, LANES))

    solved = pl.pallas_call(
        factor_kernel,
        out_shape=jax.ShapeDtypeStruct((PACK_ROWS, LANES), F32),
        in_specs=[vmem],
        out_specs=vmem,
        compiler_params=pltpu.CompilerParams(vmem_limit_bytes=big),
        name="factor",
    )(summed)

    everyone = pl.pallas_call(
        functools.partial(gather_kernel, (core, up, groups_up)),
        out_shape=jax.ShapeDtypeStruct((*dims, PACK_ROWS, LANES), F32),
        in_specs=[vmem],
        out_specs=vmem,
        scratch_shapes=[
            pltpu.SemaphoreType.DMA((count, len(up[0]), partners)),
            pltpu.SemaphoreType.DMA((count, len(up[0]), partners)),
            pltpu.SemaphoreType.DMA((count, len(up[0]), partners)),
            pltpu.SemaphoreType.DMA((count, len(up[0]), partners)),
        ],
        compiler_params=pltpu.CompilerParams(
            collective_id=1, has_side_effects=True, vmem_limit_bytes=big
        ),
        name="gather",
    )(solved).reshape(HEADS, PACK_ROWS, LANES)

    piece_rows = width // tm
    place = lax.axis_index("tm").reshape(1).astype(jnp.int32)
    leverage, zscores, pieces = pl.pallas_call(
        functools.partial(leverage_kernel, scale),
        grid=(blocks // per,),
        in_specs=[
            pl.BlockSpec(memory_space=pltpu.SMEM),
            head_spec,
            feat_spec,
            line_spec,
            pl.BlockSpec((HEADS, PACK_ROWS, LANES), lambda b: (0, 0, 0)),
        ],
        out_specs=[
            line_spec,
            pl.BlockSpec((HEADS, width), lambda b: (0, 0)),
            pl.BlockSpec((HEADS, piece_rows, width), lambda b: (0, 0, 0)),
        ],
        out_shape=[
            jax.ShapeDtypeStruct((lines, LANES), F32),
            jax.ShapeDtypeStruct((HEADS, width), F32),
            jax.ShapeDtypeStruct((HEADS, piece_rows, width), F32),
        ],
        compiler_params=pltpu.CompilerParams(vmem_limit_bytes=big),
        name="leverage",
    )(place, heads, features, weights, everyone)
    return (leverage.reshape(row_count), zscores, pieces)


def solution(mesh):
    return jax.shard_map(
        functools.partial(local, dict(mesh.shape)),
        mesh=mesh,
        in_specs=(
            P(("station", "tm"), None),
            P(("station", "tm")),
            P(("station", "tm")),
            P(("station", "tm")),
            P("station", None),
        ),
        out_specs=(P(("station", "tm")), P(), P(None, "tm", None)),
        check_vma=False,
    )
```

```python
import functools
import math

import jax
import jax.numpy as jnp
from jax import lax
from jax.experimental import pallas as pl
from jax.experimental.pallas import tpu as pltpu
from jax.sharding import PartitionSpec as P

HEADS = 16
BLK = 1024
LANES = 128
SUB = BLK // LANES
HEAD_BITS = 4
F32 = jnp.float32
HIGHEST = lax.Precision.HIGHEST
MESH = pl.DeviceIdType.MESH
PACK_ROWS = 336
VEC_ROW = 320
CHAINS = ((0, 32), (32, 32), (64, 56), (120, 48))


def bits_of(mesh_shape):
    station, tm = mesh_shape["station"], mesh_shape["tm"]
    core = ("tm", 1)
    owner = [("station", 1), ("tm", 2), ("tm", 4), ("tm", 8)]
    rest = [("station", s) for s in (2**i for i in range(1, 16)) if s < station]
    rest += [("tm", s) for s in (2**i for i in range(4, 16)) if s < tm]
    return core, owner, rest


def bit_value(bit):
    return lax.rem(lax.div(lax.axis_index(bit[0]), bit[1]), 2)


def moves_of(bits):
    return range(1, 2 ** len(bits))


def partner(bits, move):
    place = {}
    for i, (axis, step) in enumerate(bits):
        if (move >> i) & 1:
            here = place.get(axis, lax.axis_index(axis))
            place[axis] = here + (1 - 2 * bit_value((axis, step))) * step
    return place


def flipped(bit, i, move):
    value = bit_value(bit)
    return 1 - value if (move >> i) & 1 else value


def call_out(groups):
    barrier = pltpu.get_barrier_semaphore()
    met = 0
    for bits in groups:
        for move in moves_of(bits):
            pl.semaphore_signal(
                barrier, inc=1, device_id=partner(bits, move), device_id_type=MESH
            )
            met += 1
    return met


def hear(met):
    pl.semaphore_wait(pltpu.get_barrier_semaphore(), met)


def half_tiles(full):
    return full[64:128, :], full[0:64, :]


def gram_kernel(
    feat_ref, code_ref, tgt_ref, table_ref, out_ref, w_ref, acc, vec, codes, sem
):
    step = pl.program_id(0)
    per = feat_ref.shape[0] // BLK

    @pl.when(step == 0)
    def _():
        copy = pltpu.make_async_copy(code_ref, codes, sem)
        copy.start()
        acc[...] = jnp.zeros_like(acc)
        vec[...] = jnp.zeros_like(vec)
        copy.wait()

    lookup = jnp.broadcast_to(table_ref[...], (SUB, LANES))
    row = lax.broadcasted_iota(jnp.int32, (SUB, LANES), 0)
    for i in range(per):
        line = pl.multiple_of((step * per + i) * SUB, SUB)
        ids = jnp.bitwise_and(code_ref[pl.ds(line, SUB), :], LANES - 1)
        weights = jnp.take_along_axis(lookup, ids, axis=1, mode="promise_in_bounds")
        w_ref[i * SUB : (i + 1) * SUB, :] = weights
        feat = feat_ref[i * BLK : (i + 1) * BLK, :]
        turned = feat.T
        scaled = jnp.concatenate(
            [
                (turned[:, c * LANES : (c + 1) * LANES].astype(F32) * weights[c : c + 1, :]).astype(
                    jnp.bfloat16
                )
                for c in range(SUB)
            ],
            axis=1,
        )
        head = lax.div(codes[line, 0], LANES)
        acc[head] += jnp.dot(scaled, feat, preferred_element_type=F32)
        here = tgt_ref[pl.ds(line, SUB), :]
        spread = jnp.concatenate([jnp.where(row == c, here, 0.0) for c in range(SUB)], axis=1)
        vec[head] += lax.dot_general(
            spread.astype(jnp.bfloat16),
            scaled,
            (((1,), (1,)), ((), ())),
            preferred_element_type=F32,
        )

    @pl.when(step == pl.num_programs(0) - 1)
    def _():
        left = lax.broadcasted_iota(jnp.int32, (64, LANES), 1) < 64

        @pl.loop(0, HEADS, unroll=4)
        def _(h):
            g11, g22 = acc[h, 0:128, 0:128], acc[h, 128:256, 128:256]
            lower1, top1 = half_tiles(0.5 * (g11 + g11.T))
            lower2, top2 = half_tiles(0.5 * (g22 + g22.T))
            out_ref[h, 0:64, :] = jnp.where(left, top1, pltpu.roll(top2, 64, 1))
            out_ref[h, 64:128, :] = lower1
            out_ref[h, 128:192, :] = lower2
            out_ref[h, 192:320, :] = 0.5 * (acc[h, 128:256, 0:128] + acc[h, 0:128, 128:256].T)
            total = jnp.sum(vec[h], axis=0, keepdims=True)
            out_ref[h, VEC_ROW:PACK_ROWS, :] = jnp.zeros((PACK_ROWS - VEC_ROW, LANES), F32)
            out_ref[h, VEC_ROW : VEC_ROW + 1, :] = total[:, 0:128]
            out_ref[h, VEC_ROW + 1 : VEC_ROW + 2, :] = total[:, 128:256]


def reduce_kernel(plan, g_ref, out_ref, acc, first, fin, *rest):
    core_bits, orders, groups = plan
    stage_count = len(orders[0])
    count = len(CHAINS)
    bufs = [rest[c * stage_count : (c + 1) * stage_count] for c in range(count)]
    send, recv = rest[-2:]
    half = PACK_ROWS // 2
    core = bit_value(core_bits[0])
    own = [pl.ds(start, size) for start, size in CHAINS]
    mine = [pl.ds(pl.multiple_of(core * half + start, 8), size) for start, size in CHAINS]
    theirs = [pl.ds(pl.multiple_of((1 - core) * half + start, 8), size) for start, size in CHAINS]
    hear(call_out(groups))
    sent = []
    flying = [[] for _ in range(count)]
    index = [[slice(None)] * HEAD_BITS for _ in range(count)]

    def push(src, dst, chain, stage, bits, move):
        copy = pltpu.make_async_remote_copy(
            src_ref=src,
            dst_ref=dst,
            send_sem=send.at[chain, stage, move - 1],
            recv_sem=recv.at[chain, stage, move - 1],
            device_id=partner(bits, move),
            device_id_type=MESH,
        )
        copy.start()
        sent.append(copy)
        flying[chain].append(copy)

    def take(c, stage):
        arrived, flying[c] = flying[c], []
        place = (*index[c], own[c])
        for i, copy in enumerate(arrived):
            copy.wait_recv()
            if stage > 0 and not orders[c % 2][stage - 1][1]:
                copy.wait_send()
                sent[:] = [other for other in sent if other is not copy]
            if stage == 0:
                acc[place] = g_ref[:, :, :, :, mine[c], :] + first[place]
            else:
                acc[place] = acc[place] + bufs[c][stage - 1][i]

    def give(c, stage):
        if stage == stage_count:
            push(acc.at[(*index[c], own[c])], fin.at[own[c]], c, stage + 1, core_bits, 1)
            return
        bits, dims = orders[c % 2][stage]
        kept = list(index[c])
        for move in reversed(moves_of(bits)):
            away = list(index[c])
            for i, dim in enumerate(dims):
                away[dim] = flipped(bits[i], i, move)
                kept[dim] = bit_value(bits[i])
            push(acc.at[(*away, own[c])], bufs[c][stage].at[move - 1], c, stage + 1, bits, move)
        flying[c].reverse()
        index[c] = kept

    every = [slice(None)] * HEAD_BITS
    for c in range(count):
        push(g_ref.at[(*every, theirs[c])], first.at[(*every, own[c])], c, 0, core_bits, 1)
    for stage in range(stage_count + 1):
        for c in range(count):
            take(c, stage)
            give(c, stage)
    for c in range(count):
        for copy in flying[c]:
            copy.wait_recv()
        out_ref[mine[c], :] = acc[(*index[c], own[c])]
        out_ref[theirs[c], :] = fin[own[c], :]
    for copy in sent:
        copy.wait_send()


def gather_kernel(plan, g_ref, out_ref, send, recv, send_core, recv_core):
    core_bits, orders, groups = plan
    count = len(CHAINS)
    half = PACK_ROWS // 2
    core = bit_value(core_bits[0])
    mine = [pl.ds(pl.multiple_of(core * half + start, 8), size) for start, size in CHAINS]
    own = [None] * HEAD_BITS
    for bits, dims in orders[0]:
        for bit, dim in zip(bits, dims):
            own[dim] = bit_value(bit)
    met = call_out(groups)
    solve_head(g_ref, out_ref.at[(*own,)])
    hear(met)
    sent, late = [], []

    def push(place, chain, bits, move, send_sem, recv_sem):
        view = out_ref.at[(*place, mine[chain])]
        copy = pltpu.make_async_remote_copy(
            src_ref=view,
            dst_ref=view,
            send_sem=send_sem,
            recv_sem=recv_sem,
            device_id=partner(bits, move),
            device_id_type=MESH,
        )
        copy.start()
        sent.append(copy)
        return copy

    index = [list(own) for _ in range(count)]
    flying = [[] for _ in range(count)]
    stage_count = len(orders[0])

    def give(c, stage):
        if stage < stage_count:
            bits, dims = orders[c % 2][stage]
            flying[c] = [
                (
                    move,
                    push(
                        index[c],
                        c,
                        bits,
                        move,
                        send.at[c, stage, move - 1],
                        recv.at[c, stage, move - 1],
                    ),
                )
                for move in reversed(moves_of(bits))
            ]

    def take(c, stage):
        bits, dims = orders[c % 2][stage]
        fresh = []
        for move, copy in reversed(flying[c]):
            copy.wait_recv()
            news = list(index[c])
            for i, dim in enumerate(dims):
                news[dim] = flipped(bits[i], i, move)
            fresh.append((move, news))
        for dim in dims:
            index[c][dim] = slice(None)
        give(c, stage + 1)
        for move, news in fresh:
            late.append(
                push(
                    news,
                    c,
                    core_bits,
                    1,
                    send_core.at[c, stage, move - 1],
                    recv_core.at[c, stage, move - 1],
                )
            )

    turn = (2, 3, 0, 1)
    for c in turn:
        give(c, 0)
    for stage in range(stage_count):
        for c in turn:
            take(c, stage)
    for copy in late:
        copy.wait_recv()
    for copy in sent:
        copy.wait_send()


def mm(a, b, dims):
    return lax.dot_general(a, b, (dims, ((), ())), precision=HIGHEST, preferred_element_type=F32)


def eliminate(matrix, offset):
    groups = matrix.shape[0] // 8
    rows = [matrix[8 * g : 8 * g + 8, :] for g in range(groups)]
    below = lax.broadcasted_iota(jnp.int32, (8, LANES), 0)
    for p in range(groups):
        columns = [offset + 8 * p + k for k in range(8)]
        pivots = [None] * 8
        across = [[None] * 8 for _ in range(8)]
        lines = [None] * 8
        for g in range(p, groups):
            cols = [jnp.broadcast_to(rows[g][:, j : j + 1], (8, LANES)) for j in columns]
            for k in range(8):
                if g == p:
                    if k % 2 == 0:
                        a = cols[k][k : k + 1, :]
                        b = cols[k + 1][k : k + 1, :]
                        d = cols[k + 1][k + 1 : k + 2, :]
                        pivots[k] = 1.0 / a
                        pivots[k + 1] = a * (1.0 / (a * d - b * b))
                    lines[k] = rows[p][k : k + 1, :]
                    for m in range(k + 1, 8):
                        across[k][m] = cols[m][k : k + 1, :]
                factor = cols[k] * pivots[k]
                if g == p:
                    factor = jnp.where(below > k, factor, 0.0)
                for m in range(k + 1, 8):
                    cols[m] = cols[m] - factor * across[k][m]
                rows[g] = rows[g] - factor * lines[k]
    done = jnp.concatenate(rows, axis=0)
    lane = lax.broadcasted_iota(jnp.int32, done.shape, 1)
    row = lax.broadcasted_iota(jnp.int32, done.shape, 0)
    diagonal = jnp.sum(jnp.where(lane == row + offset, done, 0.0), axis=1, keepdims=True)
    return done * (1.0 / jnp.sqrt(diagonal))


def inverse_factor_128(top, bottom):
    lane = lax.broadcasted_iota(jnp.int32, (64, LANES), 1)
    row = lax.broadcasted_iota(jnp.int32, (64, LANES), 0)
    low = lane < 64
    eye = (lane == row + 64).astype(F32)
    none = jnp.zeros((64, LANES), F32)
    first = eliminate(jnp.where(low, top, eye), 0)
    x1 = jnp.where(low, pltpu.roll(first, 64, 1), 0.0)
    x1_full = jnp.concatenate([x1, none], axis=0)
    lower = mm(bottom, x1_full, ((1,), (1,)))
    square = mm(lower, jnp.concatenate([lower, none], axis=0), ((1,), (1,)))
    second = eliminate(jnp.where(low, pltpu.roll(bottom, 64, 1) - square, eye), 0)
    x2 = jnp.where(low, 0.0, second)
    across = mm(lower, x1_full, ((1,), (0,)))
    x21 = -mm(x2, jnp.concatenate([none, across], axis=0), ((1,), (0,)))
    return x1, x21 + x2


def solve_head(g_ref, out_ref):
    lane = lax.broadcasted_iota(jnp.int32, (64, LANES), 1)
    row = lax.broadcasted_iota(jnp.int32, (64, LANES), 0)
    low = lane < 64
    eye_top = (lane == row).astype(F32)
    eye_bottom = (lane == row + 64).astype(F32)
    tops = g_ref[0:64, :]
    top1, bottom1 = inverse_factor_128(tops + eye_top, g_ref[64:128, :] + eye_bottom)
    x1 = jnp.concatenate([top1, bottom1], axis=0)
    lower = mm(g_ref[192:320, :], x1, ((1,), (1,)))
    square = mm(lower, lower, ((1,), (1,)))
    top2, bottom2 = inverse_factor_128(
        pltpu.roll(tops, 64, 1) + eye_top - square[0:64, :],
        g_ref[128:192, :] + eye_bottom - square[64:128, :],
    )
    x2 = jnp.concatenate([top2, bottom2], axis=0)
    x21 = -mm(x2, mm(lower, x1, ((1,), (0,))), ((1,), (0,)))
    out_ref[0:64, :] = jnp.where(low, top1, pltpu.roll(top2, 64, 1))
    out_ref[64:128, :] = bottom1
    out_ref[128:192, :] = bottom2
    out_ref[192:320, :] = x21
    m1 = jnp.broadcast_to(g_ref[VEC_ROW : VEC_ROW + 1, :], (8, LANES))
    m2 = jnp.broadcast_to(g_ref[VEC_ROW + 1 : VEC_ROW + 2, :], (8, LANES))
    in1 = mm(m1, x1, ((1,), (1,)))
    in2 = mm(m1, x21, ((1,), (1,))) + mm(m2, x2, ((1,), (1,)))
    co1 = mm(in1, x1, ((1,), (0,))) + mm(in2, x21, ((1,), (0,)))
    co2 = mm(in2, x2, ((1,), (0,)))
    s1 = jnp.sum(x1 * x1, axis=0, keepdims=True) + jnp.sum(x21 * x21, axis=0, keepdims=True)
    s2 = jnp.sum(x2 * x2, axis=0, keepdims=True)
    out_ref[VEC_ROW:PACK_ROWS, :] = jnp.zeros((PACK_ROWS - VEC_ROW, LANES), F32)
    out_ref[VEC_ROW : VEC_ROW + 1, :] = co1[0:1, :] / jnp.sqrt(s1)
    out_ref[VEC_ROW + 1 : VEC_ROW + 2, :] = co2[0:1, :] / jnp.sqrt(s2)


def leverage_kernel(scale, place_ref, heads_ref, feat_ref, w_ref, inv_ref, lev_ref, z_ref, piece_ref):
    step = pl.program_id(0)
    per = feat_ref.shape[0] // BLK

    @pl.when(step == 0)
    def _():
        z_ref[:, 0:128] = inv_ref[:, VEC_ROW, :]
        z_ref[:, 128:256] = inv_ref[:, VEC_ROW + 1, :]
        count = piece_ref.shape[1]
        start = place_ref[0] * count
        root = math.sqrt(scale * 2 * LANES)
        low = lax.broadcasted_iota(jnp.int32, (count, LANES), 1) < 64

        def rows(first):
            return inv_ref[:, pl.ds(pl.multiple_of(first, 8), count), :] * root

        @pl.when(start < 64)
        def _():
            piece_ref[:, :, 0:128] = jnp.where(low, rows(start), 0.0)

        @pl.when(jnp.logical_and(start >= 64, start < 128))
        def _():
            piece_ref[:, :, 0:128] = rows(start)

        @pl.when(start < 128)
        def _():
            piece_ref[:, :, 128:256] = jnp.zeros((HEADS, count, LANES), F32)

        @pl.when(start >= 128)
        def _():
            piece_ref[:, :, 0:128] = rows(start + 64)

        @pl.when(jnp.logical_and(start >= 128, start < 192))
        def _():
            for h in range(HEADS):
                part = inv_ref[h, pl.ds(pl.multiple_of(start - 128, 8), count), :] * root
                piece_ref[h, :, 128:256] = jnp.where(low, pltpu.roll(part, 64, 1), 0.0)

        @pl.when(start >= 192)
        def _():
            piece_ref[:, :, 128:256] = rows(start - 64)

    low = lax.broadcasted_iota(jnp.int32, (64, LANES), 1) < 64
    zero = jnp.zeros((128, 128), jnp.bfloat16)
    for i in range(per):
        head = heads_ref[i * SUB, 0]
        tops = inv_ref[head, 0:64, :]
        x1 = jnp.concatenate([jnp.where(low, tops, 0.0), inv_ref[head, 64:128, :]], axis=0)
        x2 = jnp.concatenate(
            [jnp.where(low, pltpu.roll(tops, 64, 1), 0.0), inv_ref[head, 128:192, :]], axis=0
        )
        x21 = inv_ref[head, 192:320, :]
        x1, x21, x2 = (x.astype(jnp.bfloat16) for x in (x1, x21, x2))
        inverse = jnp.concatenate(
            [jnp.concatenate([x1, zero], axis=1), jnp.concatenate([x21, x2], axis=1)], axis=0
        )
        projected = lax.dot_general(
            feat_ref[i * BLK : (i + 1) * BLK, :],
            inverse,
            (((1,), (1,)), ((), ())),
            preferred_element_type=F32,
        )
        one, two = projected[:, 0:128], projected[:, 128:256]
        squares = one * one + two * two
        for c in range(SUB):
            line = jnp.sum(squares[c * LANES : (c + 1) * LANES, :].T, axis=0, keepdims=True)
            here = i * SUB + c
            lev_ref[here : here + 1, :] = w_ref[here : here + 1, :] * line * scale


def local(mesh_shape, features, targets, station_ids, lead_heads, station_weight):
    row_count, width = features.shape
    blocks = row_count // BLK
    lines = row_count // LANES
    tm = mesh_shape["tm"]
    total_rows = row_count * mesh_shape["station"] * tm
    scale = total_rows / (HEADS * width)
    heads = lead_heads.reshape(lines, LANES)
    codes = (lead_heads * LANES + station_ids).reshape(lines, LANES)
    goals = targets.astype(F32).reshape(lines, LANES)
    per = math.gcd(blocks, 4)
    head_spec = pl.BlockSpec((per * SUB, LANES), lambda b: (b, 0), memory_space=pltpu.SMEM)
    line_spec = pl.BlockSpec((per * SUB, LANES), lambda b: (b, 0))
    feat_spec = pl.BlockSpec((per * BLK, width), lambda b: (b, 0))
    big = 48 * 1024 * 1024
    packed, weights = pl.pallas_call(
        gram_kernel,
        grid=(blocks // per,),
        in_specs=[
            feat_spec,
            pl.BlockSpec((lines, LANES), lambda b: (0, 0)),
            pl.BlockSpec((lines, LANES), lambda b: (0, 0)),
            pl.BlockSpec((1, LANES), lambda b: (0, 0)),
        ],
        out_specs=[pl.BlockSpec((HEADS, PACK_ROWS, LANES), lambda b: (0, 0, 0)), line_spec],
        out_shape=[
            jax.ShapeDtypeStruct((HEADS, PACK_ROWS, LANES), F32),
            jax.ShapeDtypeStruct((lines, LANES), F32),
        ],
        scratch_shapes=[
            pltpu.VMEM((HEADS, width, width), F32),
            pltpu.VMEM((HEADS, 8, width), F32),
            pltpu.SMEM((lines, LANES), jnp.int32),
            pltpu.SemaphoreType.DMA,
        ],
        compiler_params=pltpu.CompilerParams(vmem_limit_bytes=big),
        name="gram",
    )(features, codes, goals, station_weight)

    core_bit, owner, rest = bits_of(mesh_shape)
    core = (core_bit,)
    x, y = ((owner[0],), (0,)), ((owner[1],), (1,))
    z = ((owner[2], owner[3]), (2, 3))
    tail = [((bit,), ()) for bit in rest]
    down = ([x, y, z] + tail, [y, x, z] + tail)
    up = ([z, y, x], [z, x, y])
    groups_up = [core] + [bits for bits, _ in up[0]]
    groups_down = groups_up + [bits for bits, _ in tail]
    partners = 3
    dims = (2,) * HEAD_BITS
    half = PACK_ROWS // 2
    count = len(CHAINS)
    buffers = []
    for c, (_, size) in enumerate(CHAINS):
        free = HEAD_BITS
        for bits, spots in down[c % 2]:
            free -= len(spots)
            shape = (len(moves_of(bits)),) + (2,) * free + (size, LANES)
            buffers.append(pltpu.VMEM(shape, F32))
    vmem = pl.BlockSpec(memory_space=pltpu.VMEM)
    summed = pl.pallas_call(
        functools.partial(reduce_kernel, (core, down, groups_down)),
        out_shape=jax.ShapeDtypeStruct((PACK_ROWS, LANES), F32),
        in_specs=[vmem],
        out_specs=vmem,
        scratch_shapes=[
            pltpu.VMEM((*dims, half, LANES), F32),
            pltpu.VMEM((*dims, half, LANES), F32),
            pltpu.VMEM((half, LANES), F32),
            *buffers,
            pltpu.SemaphoreType.DMA((count, len(down[0]) + 2, partners)),
            pltpu.SemaphoreType.DMA((count, len(down[0]) + 2, partners)),
        ],
        compiler_params=pltpu.CompilerParams(
            collective_id=0, has_side_effects=True, vmem_limit_bytes=big
        ),
        name="reduce",
    )(packed.reshape(*dims, PACK_ROWS, LANES))

    everyone = pl.pallas_call(
        functools.partial(gather_kernel, (core, up, groups_up)),
        out_shape=jax.ShapeDtypeStruct((*dims, PACK_ROWS, LANES), F32),
        in_specs=[vmem],
        out_specs=vmem,
        scratch_shapes=[
            pltpu.SemaphoreType.DMA((count, len(up[0]), partners)),
            pltpu.SemaphoreType.DMA((count, len(up[0]), partners)),
            pltpu.SemaphoreType.DMA((count, len(up[0]), partners)),
            pltpu.SemaphoreType.DMA((count, len(up[0]), partners)),
        ],
        compiler_params=pltpu.CompilerParams(
            collective_id=1, has_side_effects=True, vmem_limit_bytes=big
        ),
        name="gather",
    )(summed).reshape(HEADS, PACK_ROWS, LANES)

    piece_rows = width // tm
    place = lax.axis_index("tm").reshape(1).astype(jnp.int32)
    leverage, zscores, pieces = pl.pallas_call(
        functools.partial(leverage_kernel, scale),
        grid=(blocks // per,),
        in_specs=[
            pl.BlockSpec(memory_space=pltpu.SMEM),
            head_spec,
            feat_spec,
            line_spec,
            pl.BlockSpec((HEADS, PACK_ROWS, LANES), lambda b: (0, 0, 0)),
        ],
        out_specs=[
            line_spec,
            pl.BlockSpec((HEADS, width), lambda b: (0, 0)),
            pl.BlockSpec((HEADS, piece_rows, width), lambda b: (0, 0, 0)),
        ],
        out_shape=[
            jax.ShapeDtypeStruct((lines, LANES), F32),
            jax.ShapeDtypeStruct((HEADS, width), F32),
            jax.ShapeDtypeStruct((HEADS, piece_rows, width), F32),
        ],
        compiler_params=pltpu.CompilerParams(vmem_limit_bytes=big),
        name="leverage",
    )(place, heads, features, weights, everyone)
    return (leverage.reshape(row_count), zscores, pieces)


def solution(mesh):
    return jax.shard_map(
        functools.partial(local, dict(mesh.shape)),
        mesh=mesh,
        in_specs=(
            P(("station", "tm"), None),
            P(("station", "tm")),
            P(("station", "tm")),
            P(("station", "tm")),
            P("station", None),
        ),
        out_specs=(P(("station", "tm")), P(), P(None, "tm", None)),
        check_vma=False,
    )
```

```python
import functools
import math

import jax
import jax.numpy as jnp
from jax import lax
from jax.experimental import pallas as pl
from jax.experimental.pallas import tpu as pltpu
from jax.sharding import PartitionSpec as P

HEADS = 16
BLK = 1024
LANES = 128
SUB = BLK // LANES
HEAD_BITS = 4
F32 = jnp.float32
HIGHEST = lax.Precision.HIGHEST
MESH = pl.DeviceIdType.MESH
PACK_ROWS = 336
VEC_ROW = 320
CHAINS = ((0, 32), (32, 32), (64, 56), (120, 48))


def bits_of(mesh_shape):
    station, tm = mesh_shape["station"], mesh_shape["tm"]
    core = ("tm", 1)
    owner = [("station", 1), ("tm", 2), ("tm", 4), ("tm", 8)]
    rest = [("station", s) for s in (2**i for i in range(1, 16)) if s < station]
    rest += [("tm", s) for s in (2**i for i in range(4, 16)) if s < tm]
    return core, owner, rest


def bit_value(bit):
    return lax.rem(lax.div(lax.axis_index(bit[0]), bit[1]), 2)


def moves_of(bits):
    return range(1, 2 ** len(bits))


def partner(bits, move):
    place = {}
    for i, (axis, step) in enumerate(bits):
        if (move >> i) & 1:
            here = place.get(axis, lax.axis_index(axis))
            place[axis] = here + (1 - 2 * bit_value((axis, step))) * step
    return place


def flipped(bit, i, move):
    value = bit_value(bit)
    return 1 - value if (move >> i) & 1 else value


def call_out(groups):
    barrier = pltpu.get_barrier_semaphore()
    met = 0
    for bits in groups:
        for move in moves_of(bits):
            pl.semaphore_signal(
                barrier, inc=1, device_id=partner(bits, move), device_id_type=MESH
            )
            met += 1
    return met


def hear(met):
    pl.semaphore_wait(pltpu.get_barrier_semaphore(), met)


def half_tiles(full):
    return full[64:128, :], full[0:64, :]


def gram_kernel(
    feat_ref, code_ref, tgt_ref, table_ref, out_ref, w_ref, acc, vec, codes, sem
):
    step = pl.program_id(0)
    per = feat_ref.shape[0] // BLK

    @pl.when(step == 0)
    def _():
        copy = pltpu.make_async_copy(code_ref, codes, sem)
        copy.start()
        acc[...] = jnp.zeros_like(acc)
        vec[...] = jnp.zeros_like(vec)
        copy.wait()

    lookup = jnp.broadcast_to(table_ref[...], (SUB, LANES))
    row = lax.broadcasted_iota(jnp.int32, (SUB, LANES), 0)
    for i in range(per):
        line = pl.multiple_of((step * per + i) * SUB, SUB)
        ids = jnp.bitwise_and(code_ref[pl.ds(line, SUB), :], LANES - 1)
        weights = jnp.take_along_axis(lookup, ids, axis=1, mode="promise_in_bounds")
        w_ref[i * SUB : (i + 1) * SUB, :] = weights
        feat = feat_ref[i * BLK : (i + 1) * BLK, :]
        turned = feat.T
        scaled = jnp.concatenate(
            [
                (turned[:, c * LANES : (c + 1) * LANES].astype(F32) * weights[c : c + 1, :]).astype(
                    jnp.bfloat16
                )
                for c in range(SUB)
            ],
            axis=1,
        )
        head = lax.div(codes[line, 0], LANES)
        acc[head] += jnp.dot(scaled, feat, preferred_element_type=F32)
        here = tgt_ref[pl.ds(line, SUB), :]
        spread = jnp.concatenate([jnp.where(row == c, here, 0.0) for c in range(SUB)], axis=1)
        vec[head] += lax.dot_general(
            spread.astype(jnp.bfloat16),
            scaled,
            (((1,), (1,)), ((), ())),
            preferred_element_type=F32,
        )

    @pl.when(step == pl.num_programs(0) - 1)
    def _():
        left = lax.broadcasted_iota(jnp.int32, (64, LANES), 1) < 64

        @pl.loop(0, HEADS, unroll=4)
        def _(h):
            g11, g22 = acc[h, 0:128, 0:128], acc[h, 128:256, 128:256]
            lower1, top1 = half_tiles(0.5 * (g11 + g11.T))
            lower2, top2 = half_tiles(0.5 * (g22 + g22.T))
            out_ref[h, 0:64, :] = jnp.where(left, top1, pltpu.roll(top2, 64, 1))
            out_ref[h, 64:128, :] = lower1
            out_ref[h, 128:192, :] = lower2
            out_ref[h, 192:320, :] = 0.5 * (acc[h, 128:256, 0:128] + acc[h, 0:128, 128:256].T)
            total = jnp.sum(vec[h], axis=0, keepdims=True)
            out_ref[h, VEC_ROW:PACK_ROWS, :] = jnp.zeros((PACK_ROWS - VEC_ROW, LANES), F32)
            out_ref[h, VEC_ROW : VEC_ROW + 1, :] = total[:, 0:128]
            out_ref[h, VEC_ROW + 1 : VEC_ROW + 2, :] = total[:, 128:256]


def reduce_kernel(plan, g_ref, out_ref, acc, first, fin, *rest):
    core_bits, orders, groups = plan
    stage_count = len(orders[0])
    count = len(CHAINS)
    bufs = [rest[c * stage_count : (c + 1) * stage_count] for c in range(count)]
    send, recv = rest[-2:]
    half = PACK_ROWS // 2
    core = bit_value(core_bits[0])
    own = [pl.ds(start, size) for start, size in CHAINS]
    mine = [pl.ds(pl.multiple_of(core * half + start, 8), size) for start, size in CHAINS]
    theirs = [pl.ds(pl.multiple_of((1 - core) * half + start, 8), size) for start, size in CHAINS]
    hear(call_out(groups))
    sent = []
    flying = [[] for _ in range(count)]
    index = [[slice(None)] * HEAD_BITS for _ in range(count)]

    def push(src, dst, chain, stage, bits, move):
        copy = pltpu.make_async_remote_copy(
            src_ref=src,
            dst_ref=dst,
            send_sem=send.at[chain, stage, move - 1],
            recv_sem=recv.at[chain, stage, move - 1],
            device_id=partner(bits, move),
            device_id_type=MESH,
        )
        copy.start()
        sent.append(copy)
        flying[chain].append(copy)

    def take(c, stage):
        arrived, flying[c] = flying[c], []
        place = (*index[c], own[c])
        for i, copy in enumerate(arrived):
            copy.wait_recv()
            if stage > 0 and not orders[c % 2][stage - 1][1]:
                copy.wait_send()
                sent[:] = [other for other in sent if other is not copy]
            if stage == 0:
                acc[place] = g_ref[:, :, :, :, mine[c], :] + first[place]
            else:
                acc[place] = acc[place] + bufs[c][stage - 1][i]

    def give(c, stage):
        if stage == stage_count:
            push(acc.at[(*index[c], own[c])], fin.at[own[c]], c, stage + 1, core_bits, 1)
            return
        bits, dims = orders[c % 2][stage]
        kept = list(index[c])
        for move in reversed(moves_of(bits)):
            away = list(index[c])
            for i, dim in enumerate(dims):
                away[dim] = flipped(bits[i], i, move)
                kept[dim] = bit_value(bits[i])
            push(acc.at[(*away, own[c])], bufs[c][stage].at[move - 1], c, stage + 1, bits, move)
        flying[c].reverse()
        index[c] = kept

    every = [slice(None)] * HEAD_BITS
    for c in range(count):
        push(g_ref.at[(*every, theirs[c])], first.at[(*every, own[c])], c, 0, core_bits, 1)
    for stage in range(stage_count + 1):
        for c in range(count):
            take(c, stage)
            give(c, stage)
    for c in range(count):
        for copy in flying[c]:
            copy.wait_recv()
        out_ref[mine[c], :] = acc[(*index[c], own[c])]
        out_ref[theirs[c], :] = fin[own[c], :]
    for copy in sent:
        copy.wait_send()


def gather_kernel(plan, g_ref, out_ref, send, recv, send_core, recv_core):
    core_bits, orders, groups = plan
    count = len(CHAINS)
    half = PACK_ROWS // 2
    core = bit_value(core_bits[0])
    mine = [pl.ds(pl.multiple_of(core * half + start, 8), size) for start, size in CHAINS]
    own = [None] * HEAD_BITS
    for bits, dims in orders[0]:
        for bit, dim in zip(bits, dims):
            own[dim] = bit_value(bit)
    met = call_out(groups)
    solve_head(g_ref, out_ref.at[(*own,)])
    hear(met)
    sent, late = [], []

    def push(place, chain, bits, move, send_sem, recv_sem):
        view = out_ref.at[(*place, mine[chain])]
        copy = pltpu.make_async_remote_copy(
            src_ref=view,
            dst_ref=view,
            send_sem=send_sem,
            recv_sem=recv_sem,
            device_id=partner(bits, move),
            device_id_type=MESH,
        )
        copy.start()
        sent.append(copy)
        return copy

    index = [list(own) for _ in range(count)]
    flying = [[] for _ in range(count)]
    stage_count = len(orders[0])

    def give(c, stage):
        if stage < stage_count:
            bits, dims = orders[c % 2][stage]
            flying[c] = [
                (
                    move,
                    push(
                        index[c],
                        c,
                        bits,
                        move,
                        send.at[c, stage, move - 1],
                        recv.at[c, stage, move - 1],
                    ),
                )
                for move in reversed(moves_of(bits))
            ]

    def take(c, stage):
        bits, dims = orders[c % 2][stage]
        fresh = []
        for move, copy in reversed(flying[c]):
            copy.wait_recv()
            news = list(index[c])
            for i, dim in enumerate(dims):
                news[dim] = flipped(bits[i], i, move)
            fresh.append((move, news))
        for dim in dims:
            index[c][dim] = slice(None)
        give(c, stage + 1)
        for move, news in fresh:
            late.append(
                push(
                    news,
                    c,
                    core_bits,
                    1,
                    send_core.at[c, stage, move - 1],
                    recv_core.at[c, stage, move - 1],
                )
            )

    turn = (2, 3, 0, 1)
    for c in turn:
        give(c, 0)
    for stage in range(stage_count):
        for c in turn:
            take(c, stage)
    for copy in late:
        copy.wait_recv()
    for copy in sent:
        copy.wait_send()


def mm(a, b, dims):
    return lax.dot_general(a, b, (dims, ((), ())), precision=HIGHEST, preferred_element_type=F32)


def eliminate(matrix, offset):
    groups = matrix.shape[0] // 8
    rows = [matrix[8 * g : 8 * g + 8, :] for g in range(groups)]
    below = lax.broadcasted_iota(jnp.int32, (8, LANES), 0)
    for p in range(groups):
        columns = [offset + 8 * p + k for k in range(8)]
        pivots = [None] * 8
        across = [[None] * 8 for _ in range(8)]
        lines = [None] * 8
        for g in range(p, groups):
            cols = [jnp.broadcast_to(rows[g][:, j : j + 1], (8, LANES)) for j in columns]
            for k in range(8):
                if g == p:
                    if k % 2 == 0:
                        a = cols[k][k : k + 1, :]
                        b = cols[k + 1][k : k + 1, :]
                        d = cols[k + 1][k + 1 : k + 2, :]
                        pivots[k] = 1.0 / a
                        pivots[k + 1] = a * (1.0 / (a * d - b * b))
                    lines[k] = rows[p][k : k + 1, :]
                    for m in range(k + 1, 8):
                        across[k][m] = cols[m][k : k + 1, :]
                factor = cols[k] * pivots[k]
                if g == p:
                    factor = jnp.where(below > k, factor, 0.0)
                for m in range(k + 1, 8):
                    cols[m] = cols[m] - factor * across[k][m]
                rows[g] = rows[g] - factor * lines[k]
    done = jnp.concatenate(rows, axis=0)
    lane = lax.broadcasted_iota(jnp.int32, done.shape, 1)
    row = lax.broadcasted_iota(jnp.int32, done.shape, 0)
    diagonal = jnp.sum(jnp.where(lane == row + offset, done, 0.0), axis=1, keepdims=True)
    return done * (1.0 / jnp.sqrt(diagonal))


def inverse_factor_128(top, bottom):
    lane = lax.broadcasted_iota(jnp.int32, (64, LANES), 1)
    row = lax.broadcasted_iota(jnp.int32, (64, LANES), 0)
    low = lane < 64
    eye = (lane == row + 64).astype(F32)
    none = jnp.zeros((64, LANES), F32)
    first = eliminate(jnp.where(low, top, eye), 0)
    x1 = jnp.where(low, pltpu.roll(first, 64, 1), 0.0)
    x1_full = jnp.concatenate([x1, none], axis=0)
    lower = mm(bottom, x1_full, ((1,), (1,)))
    square = mm(lower, jnp.concatenate([lower, none], axis=0), ((1,), (1,)))
    second = eliminate(jnp.where(low, pltpu.roll(bottom, 64, 1) - square, eye), 0)
    x2 = jnp.where(low, 0.0, second)
    across = mm(lower, x1_full, ((1,), (0,)))
    x21 = -mm(x2, jnp.concatenate([none, across], axis=0), ((1,), (0,)))
    return x1, x21 + x2


def solve_head(g_ref, out_ref):
    lane = lax.broadcasted_iota(jnp.int32, (64, LANES), 1)
    row = lax.broadcasted_iota(jnp.int32, (64, LANES), 0)
    low = lane < 64
    eye_top = (lane == row).astype(F32)
    eye_bottom = (lane == row + 64).astype(F32)
    tops = g_ref[0:64, :]
    top1, bottom1 = inverse_factor_128(tops + eye_top, g_ref[64:128, :] + eye_bottom)
    x1 = jnp.concatenate([top1, bottom1], axis=0)
    lower = mm(g_ref[192:320, :], x1, ((1,), (1,)))
    square = mm(lower, lower, ((1,), (1,)))
    top2, bottom2 = inverse_factor_128(
        pltpu.roll(tops, 64, 1) + eye_top - square[0:64, :],
        g_ref[128:192, :] + eye_bottom - square[64:128, :],
    )
    x2 = jnp.concatenate([top2, bottom2], axis=0)
    x21 = -mm(x2, mm(lower, x1, ((1,), (0,))), ((1,), (0,)))
    out_ref[0:64, :] = jnp.where(low, top1, pltpu.roll(top2, 64, 1))
    out_ref[64:128, :] = bottom1
    out_ref[128:192, :] = bottom2
    out_ref[192:320, :] = x21
    m1 = jnp.broadcast_to(g_ref[VEC_ROW : VEC_ROW + 1, :], (8, LANES))
    m2 = jnp.broadcast_to(g_ref[VEC_ROW + 1 : VEC_ROW + 2, :], (8, LANES))
    in1 = mm(m1, x1, ((1,), (1,)))
    in2 = mm(m1, x21, ((1,), (1,))) + mm(m2, x2, ((1,), (1,)))
    co1 = mm(in1, x1, ((1,), (0,))) + mm(in2, x21, ((1,), (0,)))
    co2 = mm(in2, x2, ((1,), (0,)))
    s1 = jnp.sum(x1 * x1, axis=0, keepdims=True) + jnp.sum(x21 * x21, axis=0, keepdims=True)
    s2 = jnp.sum(x2 * x2, axis=0, keepdims=True)
    out_ref[VEC_ROW:PACK_ROWS, :] = jnp.zeros((PACK_ROWS - VEC_ROW, LANES), F32)
    out_ref[VEC_ROW : VEC_ROW + 1, :] = co1[0:1, :] / jnp.sqrt(s1)
    out_ref[VEC_ROW + 1 : VEC_ROW + 2, :] = co2[0:1, :] / jnp.sqrt(s2)


def leverage_kernel(scale, place_ref, heads_ref, feat_ref, w_ref, inv_ref, lev_ref, z_ref, piece_ref):
    step = pl.program_id(0)
    per = feat_ref.shape[0] // BLK

    @pl.when(step == 0)
    def _():
        z_ref[:, 0:128] = inv_ref[:, VEC_ROW, :]
        z_ref[:, 128:256] = inv_ref[:, VEC_ROW + 1, :]
        count = piece_ref.shape[1]
        start = place_ref[0] * count
        root = math.sqrt(scale * 2 * LANES)
        low = lax.broadcasted_iota(jnp.int32, (count, LANES), 1) < 64

        def rows(first):
            return inv_ref[:, pl.ds(pl.multiple_of(first, 8), count), :] * root

        @pl.when(start < 64)
        def _():
            piece_ref[:, :, 0:128] = jnp.where(low, rows(start), 0.0)

        @pl.when(jnp.logical_and(start >= 64, start < 128))
        def _():
            piece_ref[:, :, 0:128] = rows(start)

        @pl.when(start < 128)
        def _():
            piece_ref[:, :, 128:256] = jnp.zeros((HEADS, count, LANES), F32)

        @pl.when(start >= 128)
        def _():
            piece_ref[:, :, 0:128] = rows(start + 64)

        @pl.when(jnp.logical_and(start >= 128, start < 192))
        def _():
            for h in range(HEADS):
                part = inv_ref[h, pl.ds(pl.multiple_of(start - 128, 8), count), :] * root
                piece_ref[h, :, 128:256] = jnp.where(low, pltpu.roll(part, 64, 1), 0.0)

        @pl.when(start >= 192)
        def _():
            piece_ref[:, :, 128:256] = rows(start - 64)

    low = lax.broadcasted_iota(jnp.int32, (64, LANES), 1) < 64
    zero = jnp.zeros((128, 128), jnp.bfloat16)
    for i in range(per):
        head = heads_ref[i * SUB, 0]
        tops = inv_ref[head, 0:64, :]
        x1 = jnp.concatenate([jnp.where(low, tops, 0.0), inv_ref[head, 64:128, :]], axis=0)
        x2 = jnp.concatenate(
            [jnp.where(low, pltpu.roll(tops, 64, 1), 0.0), inv_ref[head, 128:192, :]], axis=0
        )
        x21 = inv_ref[head, 192:320, :]
        x1, x21, x2 = (x.astype(jnp.bfloat16) for x in (x1, x21, x2))
        inverse = jnp.concatenate(
            [jnp.concatenate([x1, zero], axis=1), jnp.concatenate([x21, x2], axis=1)], axis=0
        )
        projected = lax.dot_general(
            feat_ref[i * BLK : (i + 1) * BLK, :],
            inverse,
            (((1,), (1,)), ((), ())),
            preferred_element_type=F32,
        )
        one, two = projected[:, 0:128], projected[:, 128:256]
        squares = one * one + two * two
        for c in range(SUB):
            line = jnp.sum(squares[c * LANES : (c + 1) * LANES, :].T, axis=0, keepdims=True)
            here = i * SUB + c
            lev_ref[here : here + 1, :] = w_ref[here : here + 1, :] * line * scale


def local(mesh_shape, features, targets, station_ids, lead_heads, station_weight):
    row_count, width = features.shape
    blocks = row_count // BLK
    lines = row_count // LANES
    tm = mesh_shape["tm"]
    total_rows = row_count * mesh_shape["station"] * tm
    scale = total_rows / (HEADS * width)
    heads = lead_heads.reshape(lines, LANES)
    codes = (lead_heads * LANES + station_ids).reshape(lines, LANES)
    goals = targets.astype(F32).reshape(lines, LANES)
    per = math.gcd(blocks, 4)
    head_spec = pl.BlockSpec((per * SUB, LANES), lambda b: (b, 0), memory_space=pltpu.SMEM)
    line_spec = pl.BlockSpec((per * SUB, LANES), lambda b: (b, 0))
    feat_spec = pl.BlockSpec((per * BLK, width), lambda b: (b, 0))
    big = 48 * 1024 * 1024
    small = 20 * 1024 * 1024
    packed, weights = pl.pallas_call(
        gram_kernel,
        grid=(blocks // per,),
        in_specs=[
            feat_spec,
            pl.BlockSpec((lines, LANES), lambda b: (0, 0)),
            pl.BlockSpec((lines, LANES), lambda b: (0, 0)),
            pl.BlockSpec((1, LANES), lambda b: (0, 0)),
        ],
        out_specs=[pl.BlockSpec((HEADS, PACK_ROWS, LANES), lambda b: (0, 0, 0)), line_spec],
        out_shape=[
            jax.ShapeDtypeStruct((HEADS, PACK_ROWS, LANES), F32),
            jax.ShapeDtypeStruct((lines, LANES), F32),
        ],
        scratch_shapes=[
            pltpu.VMEM((HEADS, width, width), F32),
            pltpu.VMEM((HEADS, 8, width), F32),
            pltpu.SMEM((lines, LANES), jnp.int32),
            pltpu.SemaphoreType.DMA,
        ],
        compiler_params=pltpu.CompilerParams(vmem_limit_bytes=big),
        name="gram",
    )(features, codes, goals, station_weight)

    core_bit, owner, rest = bits_of(mesh_shape)
    core = (core_bit,)
    x, y = ((owner[0],), (0,)), ((owner[1],), (1,))
    z = ((owner[2], owner[3]), (2, 3))
    tail = [((bit,), ()) for bit in rest]
    down = ([x, y, z] + tail, [y, x, z] + tail)
    up = ([z, y, x], [z, x, y])
    groups_up = [core] + [bits for bits, _ in up[0]]
    groups_down = groups_up + [bits for bits, _ in tail]
    partners = 3
    dims = (2,) * HEAD_BITS
    half = PACK_ROWS // 2
    count = len(CHAINS)
    buffers = []
    for c, (_, size) in enumerate(CHAINS):
        free = HEAD_BITS
        for bits, spots in down[c % 2]:
            free -= len(spots)
            shape = (len(moves_of(bits)),) + (2,) * free + (size, LANES)
            buffers.append(pltpu.VMEM(shape, F32))
    vmem = pl.BlockSpec(memory_space=pltpu.VMEM)
    summed = pl.pallas_call(
        functools.partial(reduce_kernel, (core, down, groups_down)),
        out_shape=jax.ShapeDtypeStruct((PACK_ROWS, LANES), F32),
        in_specs=[vmem],
        out_specs=vmem,
        scratch_shapes=[
            pltpu.VMEM((*dims, half, LANES), F32),
            pltpu.VMEM((*dims, half, LANES), F32),
            pltpu.VMEM((half, LANES), F32),
            *buffers,
            pltpu.SemaphoreType.DMA((count, len(down[0]) + 2, partners)),
            pltpu.SemaphoreType.DMA((count, len(down[0]) + 2, partners)),
        ],
        compiler_params=pltpu.CompilerParams(
            collective_id=0, has_side_effects=True, vmem_limit_bytes=small
        ),
        name="reduce",
    )(packed.reshape(*dims, PACK_ROWS, LANES))

    everyone = pl.pallas_call(
        functools.partial(gather_kernel, (core, up, groups_up)),
        out_shape=jax.ShapeDtypeStruct((*dims, PACK_ROWS, LANES), F32),
        in_specs=[vmem],
        out_specs=vmem,
        scratch_shapes=[
            pltpu.SemaphoreType.DMA((count, len(up[0]), partners)),
            pltpu.SemaphoreType.DMA((count, len(up[0]), partners)),
            pltpu.SemaphoreType.DMA((count, len(up[0]), partners)),
            pltpu.SemaphoreType.DMA((count, len(up[0]), partners)),
        ],
        compiler_params=pltpu.CompilerParams(
            collective_id=1, has_side_effects=True, vmem_limit_bytes=small
        ),
        name="gather",
    )(summed).reshape(HEADS, PACK_ROWS, LANES)

    piece_rows = width // tm
    place = lax.axis_index("tm").reshape(1).astype(jnp.int32)
    leverage, zscores, pieces = pl.pallas_call(
        functools.partial(leverage_kernel, scale),
        grid=(blocks // per,),
        in_specs=[
            pl.BlockSpec(memory_space=pltpu.SMEM),
            head_spec,
            feat_spec,
            line_spec,
            pl.BlockSpec((HEADS, PACK_ROWS, LANES), lambda b: (0, 0, 0)),
        ],
        out_specs=[
            line_spec,
            pl.BlockSpec((HEADS, width), lambda b: (0, 0)),
            pl.BlockSpec((HEADS, piece_rows, width), lambda b: (0, 0, 0)),
        ],
        out_shape=[
            jax.ShapeDtypeStruct((lines, LANES), F32),
            jax.ShapeDtypeStruct((HEADS, width), F32),
            jax.ShapeDtypeStruct((HEADS, piece_rows, width), F32),
        ],
        compiler_params=pltpu.CompilerParams(vmem_limit_bytes=small),
        name="leverage",
    )(place, heads, features, weights, everyone)
    return (leverage.reshape(row_count), zscores, pieces)


def solution(mesh):
    return jax.shard_map(
        functools.partial(local, dict(mesh.shape)),
        mesh=mesh,
        in_specs=(
            P(("station", "tm"), None),
            P(("station", "tm")),
            P(("station", "tm")),
            P(("station", "tm")),
            P("station", None),
        ),
        out_specs=(P(("station", "tm")), P(), P(None, "tm", None)),
        check_vma=False,
    )
```
